32 devices in a mesh: lon: 8 (over z, x), lat: 4 (over y, core).
Axes of the slice: x: 2, y: 2, z: 4, core: 2. Of those that a mesh axis runs over, the one named last changes fastest.
Arguments:
- final_adjoint: float32 [4, 12, 128, 1024], P(None, None, 'lat', 'lon'), may hold values from -6 to 6
- drift_u: float32 [12, 128, 1024], P(None, 'lat', 'lon'), may hold values from -1 to 1
- drift_v: float32 [12, 128, 1024], P(None, 'lat', 'lon'), may hold values from -1 to 1
- wet_mask: int32 [12, 128, 1024], P(None, 'lat', 'lon'), may hold values 0 or 1
- bottom_level: int32 [128, 1024], P('lat', 'lon'), may hold values from 1 to 12
- viscosity: float32 [128, 1024], P('lat', 'lon'), may hold values from 0.004 to 0.02
- bulk_rate: float32 [4, 128, 1024], P(None, 'lat', 'lon'), may hold values from 0.05 to 0.3
- atmos_adjoint: float32 [3, 4, 128, 1024], P(None, None, 'lat', 'lon'), may hold values from -6 to 6
Outputs:
- start_adjoint: float32 [4, 12, 128, 1024], P(None, None, 'lat', 'lon')
- flux_adjoint: float32 [3, 4, 128, 1024], P(None, None, 'lat', 'lon')
The draws below stay inside these ranges and needn't reach their ends.
All inputs are finite; a program needn't handle non-finite values. No bound on the sum of `wet_mask` on one device may be relied on, other than what follows from the above.
Results may differ from the reference program's by a relative error of at most 0.00002.
Values sent between devices are 32-bit elements; how exact they have to be, the bound alone decides.
A program may use at most 128 MiB of HBM per device.

```python
import math
import jax
import jax.numpy as jnp

K = 12
STEPS = 3
CY = 32
CX = 128
NY = 128
NX = 1024
N_LON = 8
N_LAT = 4


def plant(drawn, own_key, low, top_value):
    extent = drawn.shape
    spot = [jax.random.randint(jax.random.fold_in(own_key, axis), (), 0, extent[axis]) for axis in range(len(extent))]
    drawn = drawn.at[tuple(spot)].set(low)
    longest = extent.index(max(extent))
    spot[longest] = (spot[longest] + 1) % extent[longest]
    return drawn.at[tuple(spot)].set(top_value)


def steps_of(rng, shape, pieces, least, high):
    gain, own = 1.0, jax.random.fold_in(rng, 6)
    for position, blocks in pieces:
        heights = jnp.exp(jax.random.uniform(jax.random.fold_in(own, position), (blocks,), jnp.float32, least / len(pieces), high / len(pieces)))
        gain = gain * jnp.repeat(heights, shape[position] // blocks).reshape([-1 if axis == position else 1 for axis in range(len(shape))])
    return gain


def normal_values(own_key, extent, spread, limit, pieces=(), kind=jnp.bfloat16):
    entries = jax.random.normal(own_key, extent, jnp.float32) * spread
    if len(pieces) > 0:
        entries = steps_of(own_key, extent, pieces, -0.22, 0.18) * entries
    return jnp.clip(entries, min=-limit, max=limit).astype(kind)


def setup_inputs(seed: int = 0) -> dict:
    key_of = jax.random.split(jax.random.key(seed), 9)
    final_adjoint = normal_values(key_of[0], (4, K, NY, NX), 1.0, 6.0, ((2, 4), (3, 8)), jnp.float32)
    drift_u = normal_values(key_of[1], (K, NY, NX), 0.25, 1.0, ((1, 4), (2, 8)), jnp.float32)
    drift_v = normal_values(key_of[2], (K, NY, NX), 0.25, 1.0, ((1, 4), (2, 8)), jnp.float32)
    wet_mask = plant((jax.random.randint(key_of[3], (K, NY, NX), 0, 5) < 4).astype(jnp.int32), jax.random.fold_in(key_of[3], 1), 0, 1)
    bottom_level = plant(jax.random.randint(key_of[4], (NY, NX), 1, K + 1), jax.random.fold_in(key_of[4], 1), 1, K).astype(jnp.int32)
    viscosity = jnp.clip(jnp.exp(math.log(0.02) - 1.6094378 * jax.random.uniform(key_of[5], (NY, NX), jnp.float32) ** steps_of(key_of[5], (NY, NX), ((0, 4), (1, 8)), -0.2, 0.2)), 0.004, 0.02)
    bulk_rate = jnp.clip(jnp.exp(math.log(0.3) - 1.7917595 * jax.random.uniform(key_of[6], (4, NY, NX), jnp.float32) ** steps_of(key_of[6], (4, NY, NX), ((1, 4), (2, 8)), -0.2, 0.2)), 0.05, 0.3)
    atmos_adjoint = normal_values(key_of[7], (STEPS, 4, NY, NX), 1.0, 6.0, ((2, 4), (3, 8)), jnp.float32)
    return dict(final_adjoint=final_adjoint, drift_u=drift_u, drift_v=drift_v, wet_mask=wet_mask, bottom_level=bottom_level, viscosity=viscosity, bulk_rate=bulk_rate, atmos_adjoint=atmos_adjoint)


lap_weight = 0.04
mixing_rate = 0.15
drag_rate = 0.2
expansion = 0.2
contraction = 0.15
pressure_weight = 0.1
coriolis_scale = 0.2

def laplace(field):
    return field[..., 2:, 1:-1] + field[..., :-2, 1:-1] + field[..., 1:-1, 2:] + field[..., 1:-1, :-2] - 4.0 * field[..., 1:-1, 1:-1]

def east_west(field):
    return 0.5 * (field[..., 1:-1, 2:] - field[..., 1:-1, :-2])

def north_south(field):
    return 0.5 * (field[..., 2:, 1:-1] - field[..., :-2, 1:-1])

def tendency_step(padded, drift_u, drift_v, wet, viscosity, coriolis, opening, bottom, damping, inner_rows):
    inner = padded[:, :, 1:-1, 1:-1]
    centre = padded[:, :, 2:-2, 2:-2]
    first = laplace(padded) * inner_rows
    biharmonic = laplace(first)
    horizontal = -(drift_u * east_west(inner) + drift_v * north_south(inner)) + lap_weight * first[:, :, 1:-1, 1:-1] - viscosity * biharmonic
    buoyancy = expansion * inner[0] - contraction * inner[1]
    pressure = pressure_weight * jnp.cumsum(buoyancy, axis=0)
    flux = opening[:-1] * (centre[:, 1:] - centre[:, :-1])
    closed = jnp.zeros_like(flux[:, :1])
    vertical = mixing_rate * (jnp.concatenate([flux, closed], axis=1) - jnp.concatenate([closed, flux], axis=1))
    zonal = centre[2]
    meridional = centre[3]
    zonal_extra = -drag_rate * bottom * zonal + coriolis * meridional - east_west(pressure)
    meridional_extra = -drag_rate * bottom * meridional - coriolis * zonal - north_south(pressure)
    nothing = jnp.zeros_like(zonal_extra)
    tendency = horizontal + vertical + jnp.stack([nothing, nothing, zonal_extra, meridional_extra])
    surface = -damping * centre[:, 0]
    tendency = tendency + jnp.concatenate([surface[:, None], jnp.zeros_like(tendency[:, 1:])], axis=1)
    return centre + wet * tendency

def reference(final_adjoint, drift_u, drift_v, wet_mask, bottom_level, viscosity, bulk_rate, atmos_adjoint):
    wet = wet_mask.astype(jnp.float32)
    level_index = jnp.arange(K, dtype=jnp.int32)[:, None, None]
    opening = (level_index + 1 < bottom_level[None]).astype(jnp.float32)
    bottom = (level_index == bottom_level[None] - 1).astype(jnp.float32)
    row_values = jnp.arange(NY, dtype=jnp.int32).astype(jnp.float32)
    coriolis = (coriolis_scale * jnp.sin(math.pi * (row_values + 0.5) / NY - math.pi / 2))[:, None]
    grid_rows = jnp.arange(NY + 2, dtype=jnp.int32)
    inner_rows = ((grid_rows >= 1) & (grid_rows <= NY)).astype(jnp.float32)[:, None]

    def advance(state):
        padded = jnp.pad(state, ((0, 0), (0, 0), (2, 2), (0, 0)))
        padded = jnp.concatenate([padded[..., -2:], padded, padded[..., :2]], axis=-1)
        return tendency_step(padded, drift_u, drift_v, wet, viscosity, coriolis, opening, bottom, bulk_rate, inner_rows)
    _, pullback = jax.vjp(advance, jnp.zeros_like(final_adjoint))
    forcing = atmos_adjoint.reshape(STEPS, 4, N_LAT, CY, N_LON, CX).transpose(0, 1, 3, 2, 5, 4).reshape(STEPS, 4, NY, NX)
    adjoint = final_adjoint
    returned = []
    for step in range(STEPS - 1, -1, -1):
        returned.append(wet[0] * adjoint[:, 0])
        adjoint = pullback(adjoint)[0]
        top = (wet[0] * bulk_rate * forcing[step])[:, None]
        adjoint = adjoint + jnp.concatenate([top, jnp.zeros_like(adjoint[:, 1:])], axis=1)
    flux_grid = jnp.stack(returned[::-1])
    flux_out = flux_grid.reshape(STEPS, 4, CY, N_LAT, CX, N_LON).transpose(0, 1, 3, 2, 5, 4).reshape(STEPS, 4, NY, NX)
    return (adjoint, flux_out)
```

```python
import math

import jax
import jax.numpy as jnp
from jax import lax
from jax.experimental import pallas as pl
from jax.experimental.pallas import tpu as pltpu
from jax.sharding import PartitionSpec as P

lap_weight = 0.04
mixing_rate = 0.15
drag_rate = 0.2
expansion = 0.2
contraction = 0.15
pressure_weight = 0.1
coriolis_scale = 0.2

MESH = pl.DeviceIdType.MESH
PAD = 8
BLOCK = 32


def roll_lanes(x, shift):
    shift = shift % x.shape[-1]
    return pltpu.roll(x, shift, x.ndim - 1) if shift else x


def east(x):
    return roll_lanes(x, -1)


def west(x):
    return roll_lanes(x, 1)


def north(x):
    return pltpu.roll(x, x.shape[0] - 1, 0)


def south(x):
    return pltpu.roll(x, 1, 0)


def make_kernel(n_lat, n_lon, fields, levels, rows, cols, window, q_share, q_pad):
    n = n_lat * n_lon
    wide = rows + 2 * PAD
    total_rows = rows * n_lat
    s_share = rows // n_lat
    lines = window * fields * s_share
    misc = 3 * levels
    groups = levels // 4

    def kernel(
        fa, du, dv, wm, bl, vi, br, at_hbm,
        out, flux,
        at, wi, bi,
        A0, A1, ST, S0, S1, SS, SC, ME, MW, RE, RW, F, FS, FE, FW, FRE, FRW,
        G, SB1, RB1, SB2, RB2,
        halo_send, halo_recv, f_send, f_recv, a2a_send, a2a_recv, in_sem,
    ):
        lat = lax.axis_index("lat")
        lon = lax.axis_index("lon")
        me = lat * n_lon + lon
        eastward = lax.rem(lon + 1, n_lon)
        westward = lax.rem(lon + n_lon - 1, n_lon)

        mid_rows = pl.ds(PAD, rows)
        loads = [
            pltpu.make_async_copy(src, dst, in_sem.at[i])
            for i, (src, dst) in enumerate([
                (at_hbm, at),
                (fa, A0.at[:, pl.ds(1, levels), mid_rows, :]),
                (du, ST.at[pl.ds(0, levels), mid_rows, :]),
                (dv, ST.at[pl.ds(levels, levels), mid_rows, :]),
                (wm, wi),
                (bl, bi),
                (vi, ST.at[misc, mid_rows, :]),
                (br, ST.at[pl.ds(misc + 2, fields), mid_rows, :]),
            ])
        ]
        for c in loads:
            c.start()

        barrier = pltpu.get_barrier_semaphore()

        @pl.loop(1, n)
        def _(k):
            other = lax.rem(me + k, n)
            pl.semaphore_signal(
                barrier, inc=1, device_id={"lat": other // n_lon, "lon": lax.rem(other, n_lon)},
                device_id_type=MESH,
            )

        lane = lax.broadcasted_iota(jnp.int32, (wide, cols), 1)
        place = lane & (BLOCK - 1)
        block = lane >> (BLOCK.bit_length() - 1)
        row = lax.broadcasted_iota(jnp.int32, (wide, cols), 0) + lat * rows - PAD
        inside = jnp.where((row >= 0) & (row < total_rows), 1.0, 0.0)
        own = slice(PAD, PAD + rows)
        low = slice(0, PAD)
        high = slice(PAD + rows, wide)

        def pack(planes):
            height = planes[0].shape[0]
            b = block[:height]
            x = roll_lanes(planes[0], -118)
            for f in range(1, 4):
                x = jnp.where(b == f, roll_lanes(planes[f], BLOCK * f - 118), x)
            return x

        def message(packed, base):
            height = packed[0].shape[0]
            p = place[:height] // 8
            x = roll_lanes(packed[0], -base)
            for j in range(1, len(packed)):
                x = jnp.where(p == j, roll_lanes(packed[j], 8 * j - base), x)
            return x

        def spread(packed, from_east, from_west, j):
            x = jnp.where(place < 10, packed, roll_lanes(packed, 12))
            x = jnp.where((place >= 10) & (place < 16), roll_lanes(from_east, 10 - 8 * j), x)
            return jnp.where((place >= 16) & (place < 22), roll_lanes(from_west, 14 - 8 * j), x)

        blank_levels = jnp.zeros((fields, 1, wide, cols), jnp.float32)
        for ref in (A0, A1):
            ref[:, 0:1] = blank_levels
            ref[:, levels + 1 : levels + 2] = blank_levels
        blank = jnp.zeros((wide, cols), jnp.float32)
        for ref in (S0, S1):
            ref[0] = blank
            ref[levels + 1] = blank

        def clear(part):
            A0[:, 1 : levels + 1, part, :] = jnp.zeros((fields, levels, PAD, cols), jnp.float32)
            ST[:, part, :] = jnp.zeros((misc + 2 + fields, PAD, cols), jnp.float32)
            F[:, part, :] = jnp.zeros((2 * fields, PAD, cols), jnp.float32)
            for ref in (RE, RW, FRE, FRW):
                ref[:, part, :] = jnp.zeros((ref.shape[0], PAD, cols), jnp.float32)

        @pl.when(lat == 0)
        def _():
            clear(low)

        @pl.when(lat == n_lat - 1)
        def _():
            clear(high)

        def statics_of(k, part):
            fourth = misc + k if k < 2 + fields else misc
            return [ST[k, part, :], ST[levels + k, part, :], ST[2 * levels + k, part, :], ST[fourth, part, :]]

        for c in loads[1:]:
            c.wait()
        for k in range(levels):
            ST[2 * levels + k, own, :] = wi[k].astype(jnp.float32)
        ST[misc + 1, own, :] = bi[...].astype(jnp.float32)

        for m in range(groups):
            packed = [pack([A0[f, 4 * m + j + 1, own, :] for f in range(4)]) for j in range(4)]
            ME[m] = message(packed, 2)
            MW[m] = message(packed, 10)
            packed = [pack(statics_of(4 * m + j, own)) for j in range(4)]
            ME[groups + m] = message(packed, 2)
            MW[groups + m] = message(packed, 10)

        def transposed(x):
            if x.shape[0] < cols:
                x = jnp.concatenate([x, jnp.zeros((cols - x.shape[0], cols), x.dtype)], axis=0)
            return x.T

        loads[0].wait()
        for b in range(n_lat):
            x = at[:, :, b * s_share : (b + 1) * s_share, :].reshape(lines, cols)
            t = transposed(x)
            for a in range(n_lon):
                at_row = (b * n_lon + a) * q_pad
                SB1[at_row : at_row + q_share, :] = t[a * q_share : (a + 1) * q_share]

        pl.semaphore_wait(barrier, n - 1)

        def remote(src, dst, send, recv, i, to_lat, to_lon):
            return pltpu.make_async_remote_copy(
                src_ref=src, dst_ref=dst, send_sem=send.at[i], recv_sem=recv.at[i],
                device_id={"lat": to_lat, "lon": to_lon}, device_id_type=MESH,
            )

        def strip_copies(to_e, to_w, from_e, from_w, send, recv, i):
            mid = pl.ds(PAD, rows)
            both = [
                remote(to_e, from_w.at[:, mid, :], send, recv, i, lat, eastward),
                remote(to_w, from_e.at[:, mid, :], send, recv, i + 1, lat, westward),
            ]
            top, bottom = pl.ds(rows - PAD, PAD), pl.ds(0, PAD)
            up = [
                remote(to_e.at[:, top, :], from_w.at[:, low, :], send, recv, i + 2, lat + 1, eastward),
                remote(to_w.at[:, top, :], from_e.at[:, low, :], send, recv, i + 3, lat + 1, westward),
            ]
            down = [
                remote(to_e.at[:, bottom, :], from_w.at[:, high, :], send, recv, i + 4, lat - 1, eastward),
                remote(to_w.at[:, bottom, :], from_e.at[:, high, :], send, recv, i + 5, lat - 1, westward),
            ]
            return both, up, down

        def start(copies):
            both, up, down = copies
            for c in both:
                c.start()

            @pl.when(lat < n_lat - 1)
            def _():
                for c in up:
                    c.start()

            @pl.when(lat > 0)
            def _():
                for c in down:
                    c.start()

        def finish_recv(copies):
            both, up, down = copies
            for c in both:
                c.wait_recv()

            @pl.when(lat > 0)
            def _():
                for c in up:
                    c.wait_recv()

            @pl.when(lat < n_lat - 1)
            def _():
                for c in down:
                    c.wait_recv()

        def finish_send(copies):
            both, up, down = copies
            for c in both:
                c.wait_send()

            @pl.when(lat < n_lat - 1)
            def _():
                for c in up:
                    c.wait_send()

            @pl.when(lat > 0)
            def _():
                for c in down:
                    c.wait_send()

        def place_of(device):
            return pl.ds(pl.multiple_of(device * q_pad, 8), q_pad)

        def exchange(src, dst, i):
            @pl.loop(1, n)
            def _(k):
                other = lax.rem(me + k, n)
                pltpu.make_async_remote_copy(
                    src_ref=src.at[place_of(other)], dst_ref=dst.at[place_of(me)],
                    send_sem=a2a_send.at[i], recv_sem=a2a_recv.at[i],
                    device_id={"lat": other // n_lon, "lon": lax.rem(other, n_lon)},
                    device_id_type=MESH,
                ).start()

            dst[place_of(me), :] = src[place_of(me), :]

        def all_of(src, dst, sem):
            some = pl.ds(0, (n - 1) * q_pad)
            return pltpu.make_async_copy(src.at[some], dst.at[some], sem)

        both, up, down = strip_copies(ME, MW, RE, RW, halo_send, halo_recv, 0)
        inner = pl.ds(1, levels)
        up = up + [
            remote(A0.at[:, inner, pl.ds(rows, PAD), :], A0.at[:, inner, low, :],
                   halo_send, halo_recv, 6, lat + 1, lon),
            remote(ST.at[:, pl.ds(rows, PAD), :], ST.at[:, low, :],
                   halo_send, halo_recv, 7, lat + 1, lon),
        ]
        down = down + [
            remote(A0.at[:, inner, pl.ds(PAD, PAD), :], A0.at[:, inner, high, :],
                   halo_send, halo_recv, 8, lat - 1, lon),
            remote(ST.at[:, pl.ds(PAD, PAD), :], ST.at[:, high, :],
                   halo_send, halo_recv, 9, lat - 1, lon),
        ]
        halo = (both, up, down)
        start(halo)
        exchange(SB1, RB1, 0)

        finish_recv(halo)
        everywhere = slice(0, wide)

        def replicate(x, g):
            x = jnp.where(block == g, x, 0.0)
            x = x + roll_lanes(x, 2 * BLOCK)
            return x + roll_lanes(x, BLOCK)

        rate = blank
        for k in range(levels):
            m, j = k // 4, k % 4
            S0[k + 1] = spread(pack([A0[f, k + 1] for f in range(4)]), RE[m], RW[m], j)
            x = spread(pack(statics_of(k, everywhere)), RE[groups + m], RW[groups + m], j)
            for g in range(3):
                SS[g * levels + k] = replicate(x, g)
            if k < 2:
                SC[k] = replicate(x, 3)
            elif k < 2 + fields:
                f = k - 2
                rate = jnp.where(block == f, roll_lanes(x, BLOCK * (f - 3)), rate)
        SC[2] = rate

        all_of(SB1, RB1, a2a_recv.at[0]).wait()
        for b in range(n_lat):
            parts = []
            for q in range(q_share):
                parts.append(RB1[pl.ds(b * n_lon * q_pad + q, n_lon, stride=q_pad), :])
            t = jnp.concatenate(parts, axis=0).T
            G[pl.ds(b, lines, stride=n_lat), :] = t[:lines]
        for i, step in ((0, 2), (1, 1)):
            for f in range(fields):
                at_row = (step * fields + f) * rows
                F[i * fields + f, own, :] = G[at_row : at_row + rows]
        packed = [pack([F[i * fields + f, own, :] for f in range(4)]) for i in range(2)]
        FE[0] = message(packed, 2)
        FW[0] = message(packed, 10)
        both, up, down = strip_copies(FE, FW, FRE, FRW, f_send, f_recv, 0)
        up = up + [remote(F.at[:, pl.ds(rows, PAD), :], F.at[:, low, :], f_send, f_recv, 6, lat + 1, lon)]
        down = down + [remote(F.at[:, pl.ds(PAD, PAD), :], F.at[:, high, :], f_send, f_recv, 7, lat - 1, lon)]
        f_halo = (both, up, down)
        start(f_halo)

        angle = math.pi * (row.astype(jnp.float32) + 0.5) / total_rows - math.pi / 2
        SC[3] = coriolis_scale * jnp.sin(angle)
        SC[4] = inside

        half_t = 0.5 * pressure_weight * expansion
        half_s = -0.5 * pressure_weight * contraction
        edge = (lane < 2) | (lane >= cols - 2)

        def laplace(x):
            return (east(x) + west(x)) + (north(x) + south(x)) - 4.0 * x

        def spatial(w, u, v, extra_u, extra_v, visc, mask):
            x = (lap_weight * w - laplace(visc * w)) * mask
            hw = 0.5 * w
            along, across = u * hw, v * hw
            if extra_u is not None:
                along, across = along + extra_u, across + extra_v
            return (
                (east(x + along) + west(x - along))
                + (north(x + across) + south(x - across))
                - 4.0 * x
            )

        def advance(A, S, B, R):
            def body(i, carry):
                cu, cv, cs = carry
                k = levels - 1 - i
                kf = k.astype(jnp.float32)
                lower = kf + jnp.where(k == 0, 1000.0, 0.0)
                mask, cor = SC[4], SC[3]

                depth = SC[1]
                visc = SC[0]
                wet = SS[2 * levels + k]
                up_wet = SS[2 * levels + jnp.where(k == 0, 0, k - 1)]
                down_wet = SS[2 * levels + jnp.where(k == levels - 1, k, k + 1)]
                a = S[k + 1]
                w = wet * a
                cs = cs + w
                c32, c64, c96 = roll_lanes(cs, 32), roll_lanes(cs, 64), roll_lanes(cs, 96)
                extra_u = jnp.where(block == 0, half_t * c64, jnp.where(block == 1, half_s * c96, 0.0))
                extra_v = jnp.where(block == 0, half_t * c32, jnp.where(block == 1, half_s * c64, 0.0))
                new = a + spatial(w, SS[k], SS[levels + k], extra_u, extra_v, visc, mask)
                new = new + jnp.where(depth > kf + 1.0, mixing_rate, 0.0) * (down_wet * S[k + 2] - w)
                new = new - jnp.where(depth > lower, mixing_rate, 0.0) * (w - up_wet * S[k])
                new = new - jnp.where((depth == kf + 1.0) & (block >= 2), drag_rate, 0.0) * w
                new = new + cor * jnp.where(
                    block == 3, roll_lanes(w, 32), jnp.where(block == 2, -roll_lanes(w, 96), 0.0)
                )
                R[k + 1] = new
                joined = jnp.where(place < 10, new, roll_lanes(new, -12))

                depth = ST[misc + 1]
                visc = ST[misc]
                wet = ST[2 * levels + k]
                up_wet = ST[2 * levels + jnp.where(k == 0, 0, k - 1)]
                down_wet = ST[2 * levels + jnp.where(k == levels - 1, k, k + 1)]
                mix_down = jnp.where(depth > kf + 1.0, mixing_rate, 0.0)
                mix_up = jnp.where(depth > lower, mixing_rate, 0.0)
                drag = jnp.where(depth == kf + 1.0, drag_rate, 0.0)
                wu = wet * A[2, k + 1]
                wv = wet * A[3, k + 1]
                cu = cu + wu
                cv = cv + wv
                for f in range(4):
                    a = A[f, k + 1]
                    w = (wet * a, wet * a, wu, wv)[f]
                    h = (half_t, half_s, 0.0, 0.0)[f]
                    eu = h * cu if f < 2 else None
                    ev = h * cv if f < 2 else None
                    new = a + spatial(w, ST[k], ST[levels + k], eu, ev, visc, mask)
                    new = new + mix_down * (down_wet * A[f, k + 2] - w)
                    new = new - mix_up * (w - up_wet * A[f, k])
                    if f == 2:
                        new = new - drag * w - cor * wv
                    if f == 3:
                        new = new - drag * w + cor * wu
                    B[f, k + 1] = jnp.where(edge, roll_lanes(joined, 118 - BLOCK * f), new)
                return cu, cv, cs

            lax.fori_loop(0, levels, body, (blank, blank, blank))

        wet_top = 2 * levels

        for f in range(fields):
            at_row = (2 * fields + f) * rows
            flux_rows = A0[f, 1, own, :] * ST[wet_top, own, :]
            G[at_row : at_row + rows] = flux_rows

        advance(A0, S0, A1, S1)
        finish_send(halo)
        finish_recv(f_halo)
        for i in range(2):
            x = pack([F[i * fields + f] for f in range(4)])
            FS[i] = spread(x, FRE[0], FRW[0], i)

        def surface(A, S, B, R, i):
            R[1] = R[1] + SS[wet_top] * SC[2] * (FS[i] - S[1])
            for f in range(fields):
                gain = ST[wet_top] * ST[misc + 2 + f]
                B[f, 1] = B[f, 1] + gain * (F[i * fields + f] - A[f, 1])

        def store_flux(A, step):
            for f in range(fields):
                at_row = (step * fields + f) * rows
                G[at_row : at_row + rows] = A[f, 1, own, :] * ST[wet_top, own, :]

        surface(A0, S0, A1, S1, 0)
        store_flux(A1, 1)
        advance(A1, S1, A0, S0)
        surface(A1, S1, A0, S0, 1)

        finish_send(f_halo)
        last = [G[f * rows : (f + 1) * rows] for f in range(fields)]
        for f in range(fields):
            F[f, own, :] = last[f]
        store_flux(A0, 0)
        for b in range(n_lat):
            t = transposed(G[pl.ds(b, lines, stride=n_lat), :])
            for q in range(q_share):
                SB2[pl.ds(b * n_lon * q_pad + q, n_lon, stride=q_pad), :] = t[q * n_lon : (q + 1) * n_lon]
        exchange(SB2, RB2, 1)

        advance(A0, S0, A1, S1)
        for f in range(fields):
            gain = ST[wet_top, own, :] * ST[misc + 2 + f, own, :]
            A1[f, 1, own, :] = A1[f, 1, own, :] + gain * (F[f, own, :] - A0[f, 1, own, :])
        out[...] = A1[:, 1 : levels + 1, own, :]

        all_of(SB2, RB2, a2a_recv.at[1]).wait()
        for b in range(n_lat):
            starts = [(b * n_lon + a) * q_pad for a in range(n_lon)]
            x = jnp.concatenate([RB2[i : i + q_share, :] for i in starts], axis=0)
            t = x.T[:lines]
            flux[:, :, b * s_share : (b + 1) * s_share, :] = t.reshape(window, fields, s_share, cols)
        all_of(SB1, RB1, a2a_send.at[0]).wait()
        all_of(SB2, RB2, a2a_send.at[1]).wait()

    return kernel


def local(
    final_adjoint, drift_u, drift_v, wet_mask, bottom_level, viscosity, bulk_rate, atmos_adjoint
):
    fields, levels, rows, cols = final_adjoint.shape
    window = atmos_adjoint.shape[0]
    n_lat, n_lon = lax.axis_size("lat"), lax.axis_size("lon")
    n = n_lat * n_lon
    wide = rows + 2 * PAD
    q_share = cols // n_lon
    q_pad = -(-q_share // 8) * 8
    groups = levels // 4

    def buf(*shape):
        return pltpu.VMEM(shape, jnp.float32)

    kernel = make_kernel(n_lat, n_lon, fields, levels, rows, cols, window, q_share, q_pad)
    f32 = jnp.float32
    anywhere = pl.BlockSpec(memory_space=pl.ANY)
    return pl.pallas_call(
        kernel,
        out_shape=(
            pltpu.VMEM(final_adjoint.shape, f32),
            pltpu.VMEM(atmos_adjoint.shape, f32),
        ),
        in_specs=[anywhere] * 8,
        out_specs=(pl.BlockSpec(memory_space=pltpu.VMEM),) * 2,
        scratch_shapes=[
            buf(window, fields, rows, cols),
            pltpu.VMEM((levels, rows, cols), jnp.int32), pltpu.VMEM((rows, cols), jnp.int32),
            buf(fields, levels + 2, wide, cols), buf(fields, levels + 2, wide, cols),
            buf(3 * levels + 2 + fields, wide, cols),
            buf(levels + 2, wide, cols), buf(levels + 2, wide, cols),
            buf(3 * levels, wide, cols), buf(5, wide, cols),
            buf(2 * groups, rows, cols), buf(2 * groups, rows, cols),
            buf(2 * groups, wide, cols), buf(2 * groups, wide, cols),
            buf(2 * fields, wide, cols), buf(2, wide, cols),
            buf(1, rows, cols), buf(1, rows, cols), buf(1, wide, cols), buf(1, wide, cols),
            buf(window * fields * rows, cols),
            buf(n * q_pad, cols), buf(n * q_pad, cols), buf(n * q_pad, cols), buf(n * q_pad, cols),
            pltpu.SemaphoreType.DMA((10,)), pltpu.SemaphoreType.DMA((10,)),
            pltpu.SemaphoreType.DMA((8,)), pltpu.SemaphoreType.DMA((8,)),
            pltpu.SemaphoreType.DMA((2,)), pltpu.SemaphoreType.DMA((2,)), pltpu.SemaphoreType.DMA((8,)),
        ],
        compiler_params=pltpu.CompilerParams(
            collective_id=0, has_side_effects=True, vmem_limit_bytes=60 * 1024 * 1024
        ),
    )(final_adjoint, drift_u, drift_v, wet_mask, bottom_level, viscosity, bulk_rate, atmos_adjoint)


def solution(mesh):
    in_specs = (
        P(None, None, "lat", "lon"),
        P(None, "lat", "lon"),
        P(None, "lat", "lon"),
        P(None, "lat", "lon"),
        P("lat", "lon"),
        P("lat", "lon"),
        P(None, "lat", "lon"),
        P(None, None, "lat", "lon"),
    )
    out_specs = (P(None, None, "lat", "lon"), P(None, None, "lat", "lon"))
    return jax.shard_map(local, mesh=mesh, in_specs=in_specs, out_specs=out_specs, check_vma=False)
```

```python
import math

import jax
import jax.numpy as jnp
from jax import lax
from jax.experimental import pallas as pl
from jax.experimental.pallas import tpu as pltpu
from jax.sharding import PartitionSpec as P

lap_weight = 0.04
mixing_rate = 0.15
drag_rate = 0.2
expansion = 0.2
contraction = 0.15
pressure_weight = 0.1
coriolis_scale = 0.2

MESH = pl.DeviceIdType.MESH
PAD = 8
BLOCK = 32
UNROLL = 3


def roll_lanes(x, shift):
    shift = shift % x.shape[-1]
    return pltpu.roll(x, shift, x.ndim - 1) if shift else x


def east(x):
    return roll_lanes(x, -1)


def west(x):
    return roll_lanes(x, 1)


def north(x):
    return pltpu.roll(x, x.shape[0] - 1, 0)


def south(x):
    return pltpu.roll(x, 1, 0)


def make_kernel(n_lat, n_lon, fields, levels, rows, cols, window, q_share, q_pad):
    n = n_lat * n_lon
    wide = rows + 2 * PAD
    total_rows = rows * n_lat
    s_share = rows // n_lat
    lines = window * fields * s_share
    misc = 3 * levels
    groups = levels // 4
    strips = (fields + 3) * groups + 2
    messages = -(-strips // 4)

    def kernel(
        fa, du, dv, wm, bl, vi, br, at_hbm,
        out, flux,
        at, A0, A1, ST, WI, BI, SP, SN, SC, SG, J, ME, MW, RE, RW, F, FS, FE, FW, FRE, FRW,
        G, H, SB1, RB1, SB2, RB2,
        halo_send, halo_recv, side_send, side_recv, f_send, f_recv, a2a_send, a2a_recv, in_sem,
    ):
        lat = lax.axis_index("lat")
        lon = lax.axis_index("lon")
        me = lat * n_lon + lon
        eastward = lax.rem(lon + 1, n_lon)
        westward = lax.rem(lon + n_lon - 1, n_lon)

        mid_rows = pl.ds(PAD, rows)
        inner = pl.ds(1, levels)
        loads = [
            pltpu.make_async_copy(src, dst, in_sem.at[i])
            for i, (src, dst) in enumerate([
                (at_hbm, at),
                (fa, A0.at[:, inner, mid_rows, :]),
                (du, ST.at[pl.ds(0, levels), mid_rows, :]),
                (dv, ST.at[pl.ds(levels, levels), mid_rows, :]),
                (wm, WI.at[:, mid_rows, :]),
                (bl, BI.at[mid_rows, :]),
                (vi, ST.at[misc, mid_rows, :]),
                (br, ST.at[pl.ds(misc + 2, fields), mid_rows, :]),
            ])
        ]
        for c in loads:
            c.start()

        barrier = pltpu.get_barrier_semaphore()

        @pl.loop(1, n)
        def _(k):
            other = lax.rem(me + k, n)
            pl.semaphore_signal(
                barrier, inc=1, device_id={"lat": other // n_lon, "lon": lax.rem(other, n_lon)},
                device_id_type=MESH,
            )

        lane = lax.broadcasted_iota(jnp.int32, (wide, cols), 1)
        place = lane & (BLOCK - 1)
        block = lane >> (BLOCK.bit_length() - 1)
        row = lax.broadcasted_iota(jnp.int32, (wide, cols), 0) + lat * rows - PAD
        own = slice(PAD, PAD + rows)
        low = slice(0, PAD)
        high = slice(PAD + rows, wide)
        everything = slice(0, wide)

        def pack(planes):
            height = planes[0].shape[0]
            b = block[:height]
            x = roll_lanes(planes[0], -118)
            for f in range(1, 4):
                x = jnp.where(b == f, roll_lanes(planes[f], BLOCK * f - 118), x)
            return x

        def message(packed, base):
            height = packed[0].shape[0]
            p = place[:height] // 8
            x = roll_lanes(packed[0], -base)
            for j in range(1, len(packed)):
                x = jnp.where(p == j, roll_lanes(packed[j], 8 * j - base), x)
            return x

        def lay(packed):
            return jnp.where(place[: packed.shape[0]] < 10, packed, roll_lanes(packed, 12))

        for ref in (A0, A1):
            ref[:, 0:1] = jnp.zeros((fields, 1, wide, cols), jnp.float32)

        def clear(part):
            A0[:, 1 : levels + 1, part, :] = jnp.zeros((fields, levels, PAD, cols), jnp.float32)
            ST[:, part, :] = jnp.zeros((misc + 2 + fields, PAD, cols), jnp.float32)
            WI[:, part, :] = jnp.zeros((levels, PAD, cols), jnp.int32)
            BI[part, :] = jnp.zeros((PAD, cols), jnp.int32)
            F[:, part, :] = jnp.zeros((2 * fields, PAD, cols), jnp.float32)
            for ref in (RE, RW, FRE, FRW):
                ref[:, part, :] = jnp.zeros((ref.shape[0], PAD, cols), jnp.float32)

        @pl.when(lat == 0)
        def _():
            clear(low)

        @pl.when(lat == n_lat - 1)
        def _():
            clear(high)

        angle = math.pi * (row.astype(jnp.float32) + 0.5) / total_rows - math.pi / 2
        SC[2] = coriolis_scale * jnp.sin(angle)

        def remote(src, dst, send, recv, i, to_lat, to_lon):
            return pltpu.make_async_remote_copy(
                src_ref=src, dst_ref=dst, send_sem=send.at[i], recv_sem=recv.at[i],
                device_id={"lat": to_lat, "lon": to_lon}, device_id_type=MESH,
            )

        def strip_copies(to_e, to_w, from_e, from_w, send, recv):
            both = [
                remote(to_e, from_w.at[:, mid_rows, :], send, recv, 0, lat, eastward),
                remote(to_w, from_e.at[:, mid_rows, :], send, recv, 1, lat, westward),
            ]
            top, bottom = pl.ds(rows - PAD, PAD), pl.ds(0, PAD)
            up = [
                remote(to_e.at[:, top, :], from_w.at[:, low, :], send, recv, 2, lat + 1, eastward),
                remote(to_w.at[:, top, :], from_e.at[:, low, :], send, recv, 3, lat + 1, westward),
            ]
            down = [
                remote(to_e.at[:, bottom, :], from_w.at[:, high, :], send, recv, 4, lat - 1, eastward),
                remote(to_w.at[:, bottom, :], from_e.at[:, high, :], send, recv, 5, lat - 1, westward),
            ]
            return both, up, down

        def start(copies):
            both, up, down = copies
            for c in both:
                c.start()

            @pl.when(lat < n_lat - 1)
            def _():
                for c in up:
                    c.start()

            @pl.when(lat > 0)
            def _():
                for c in down:
                    c.start()

        def finish_recv(copies):
            both, up, down = copies
            for c in both:
                c.wait_recv()

            @pl.when(lat > 0)
            def _():
                for c in up:
                    c.wait_recv()

            @pl.when(lat < n_lat - 1)
            def _():
                for c in down:
                    c.wait_recv()

        def finish_send(copies):
            both, up, down = copies
            for c in both:
                c.wait_send()

            @pl.when(lat < n_lat - 1)
            def _():
                for c in up:
                    c.wait_send()

            @pl.when(lat > 0)
            def _():
                for c in down:
                    c.wait_send()

        def rims(to, start_row, i, to_lat):
            src, dst = pl.ds(start_row, PAD), to
            return [
                remote(fa.at[:, :, src, :], A0.at[:, inner, dst, :], halo_send, halo_recv, i, to_lat, lon),
                remote(du.at[:, src, :], ST.at[pl.ds(0, levels), dst, :], halo_send, halo_recv, i + 1, to_lat, lon),
                remote(dv.at[:, src, :], ST.at[pl.ds(levels, levels), dst, :], halo_send, halo_recv, i + 2, to_lat, lon),
                remote(wm.at[:, src, :], WI.at[:, dst, :], halo_send, halo_recv, i + 3, to_lat, lon),
                remote(bl.at[src, :], BI.at[dst, :], halo_send, halo_recv, i + 4, to_lat, lon),
                remote(vi.at[src, :], ST.at[misc, dst, :], halo_send, halo_recv, i + 5, to_lat, lon),
                remote(br.at[:, src, :], ST.at[pl.ds(misc + 2, fields), dst, :], halo_send, halo_recv, i + 6, to_lat, lon),
            ]

        halo = ([], rims(low, rows - PAD, 0, lat + 1), rims(high, 0, 7, lat - 1))
        side = strip_copies(ME, MW, RE, RW, side_send, side_recv)

        pl.semaphore_wait(barrier, n - 1)
        start(halo)

        def convert(part):
            for k in range(levels):
                ST[k, part, :] = 0.5 * ST[k, part, :]
                ST[levels + k, part, :] = 0.5 * ST[levels + k, part, :]
                ST[2 * levels + k, part, :] = WI[k, part, :].astype(jnp.float32)
            ST[misc + 1, part, :] = BI[part, :].astype(jnp.float32)

        def sources(i, part):
            if i < fields * groups:
                f, j = divmod(i, groups)
                return [A0[f, b * groups + j + 1, part, :] for b in range(4)]
            if i < (fields + 3) * groups:
                kind, j = divmod(i - fields * groups, groups)
                return [ST[kind * levels + b * groups + j, part, :] for b in range(4)]
            if i == (fields + 3) * groups:
                v, d = ST[misc, part, :], ST[misc + 1, part, :]
                return [v, d, v, d]
            return [ST[misc + 2 + f, part, :] for f in range(4)]

        for c in loads[1:]:
            c.wait()
        convert(own)
        for m in range(messages):
            ids = range(4 * m, min(4 * m + 4, strips))
            packed = [pack(sources(i, own)) for i in ids]
            ME[m] = message(packed, 4)
            MW[m] = message(packed, 10)
            for i, x in zip(ids, packed):
                SP[i, own, :] = lay(x)
        start(side)

        def transposed(x):
            if x.shape[0] < cols:
                x = jnp.concatenate([x, jnp.zeros((cols - x.shape[0], cols), x.dtype)], axis=0)
            return x.T

        loads[0].wait()
        for b in range(n_lat):
            x = at[:, :, b * s_share : (b + 1) * s_share, :].reshape(lines, cols)
            t = transposed(x)
            for a in range(n_lon):
                at_row = (b * n_lon + a) * q_pad
                SB1[at_row : at_row + q_share, :] = t[a * q_share : (a + 1) * q_share]

        def place_of(device):
            return pl.ds(pl.multiple_of(device * q_pad, 8), q_pad)

        def exchange(src, dst, i):
            @pl.loop(1, n)
            def _(k):
                other = lax.rem(me + k, n)
                pltpu.make_async_remote_copy(
                    src_ref=src.at[place_of(other)], dst_ref=dst.at[place_of(me)],
                    send_sem=a2a_send.at[i], recv_sem=a2a_recv.at[i],
                    device_id={"lat": other // n_lon, "lon": lax.rem(other, n_lon)},
                    device_id_type=MESH,
                ).start()

            dst[place_of(me), :] = src[place_of(me), :]

        def all_of(src, dst, sem):
            some = pl.ds(0, (n - 1) * q_pad)
            return pltpu.make_async_copy(src.at[some], dst.at[some], sem)

        exchange(SB1, RB1, 0)

        finish_recv(halo)
        for part in (low, high):
            convert(part)
            for i in range(strips):
                SP[i, part, :] = lay(pack(sources(i, part)))

        finish_recv(side)
        between = (place >= 10) & (place < 22)
        half = lane & 15
        for m in range(messages):
            from_e, from_w = RE[m], roll_lanes(RW[m], 6)
            even = jnp.where(half < 6, from_e, from_w)
            odd = jnp.where((half >= 8) & (half < 14), from_e, from_w)
            for p in range(min(4, strips - 4 * m)):
                x = roll_lanes((even, odd)[p % 2], 10 - 8 * p)
                SP[4 * m + p] = jnp.where(between, x, SP[4 * m + p])

        strip_u, strip_v, strip_wet = [(fields + i) * groups for i in range(3)]
        x = SP[(fields + 3) * groups]
        SC[0] = jnp.where((block & 1) == 0, x, roll_lanes(x, BLOCK))
        SC[1] = jnp.where((block & 1) == 1, x, roll_lanes(x, -BLOCK)) - (block * groups).astype(jnp.float32)
        x = SP[(fields + 3) * groups + 1]
        for f in range(fields):
            SG[f] = jnp.where(block == 0, SP[strip_wet] * roll_lanes(x, -BLOCK * f), 0.0)

        half_t = 0.5 * pressure_weight * expansion
        half_s = -0.5 * pressure_weight * contraction
        edge2 = (lane < 2) | (lane >= cols - 2)
        edge4 = (lane < 4) | (lane >= cols - 4)
        keep_low = jnp.where(lat > 0, 1.0, 0.0)
        keep_high = jnp.where(lat < n_lat - 1, 1.0, 0.0)

        def masked(x):
            return jnp.concatenate([x[low] * keep_low, x[own], x[high] * keep_high], axis=0)

        def spatial(w, u, v, extra_u, extra_v, visc, part):
            y = visc * w
            inner_lap = (north(y) + south(y)) - 4.0 * y
            z = lap_weight * w - masked(inner_lap)
            along, across = u * w, v * w
            if extra_u is not None:
                along, across = along + extra_u, across + extra_v
            vertical = north(z + across) + south(z - across)
            z, y, along = z[part], y[part], along[part]
            t = z - inner_lap[part]
            flat = (east(t + along) + west(t - along)) - (roll_lanes(y, -2) + roll_lanes(y, 2))
            return (flat + vertical[part]) - (4.0 * z + 2.0 * y)

        def strip_step(A, B):
            depth, visc, cor = SC[1], SC[0], SC[2]
            w = [[SP[strip_wet + j] * A[f * groups + j] for j in range(groups)] for f in range(fields)]
            sums = []
            for f in (2, 3):
                c = [w[f][groups - 1]]
                for j in range(groups - 2, -1, -1):
                    c.insert(0, c[0] + w[f][j])
                later = 0.0
                for b in range(1, 4):
                    later = later + jnp.where(block < 4 - b, roll_lanes(c[0], -BLOCK * b), 0.0)
                sums.append([x + later for x in c])
            down = []
            for j in range(groups):
                mix = jnp.where(depth > j + 1.0, mixing_rate, 0.0)
                down.append([
                    mix * ((w[f][j + 1] if j < groups - 1 else roll_lanes(w[f][0], -BLOCK)) - w[f][j])
                    for f in range(fields)
                ])
            for j in range(groups):
                drag = jnp.where(depth == j + 1.0, drag_rate, 0.0)
                u, v = SP[strip_u + j], SP[strip_v + j]
                for f in range(fields):
                    h = (half_t, half_s, 0.0, 0.0)[f]
                    eu = h * sums[0][j] if f < 2 else None
                    ev = h * sums[1][j] if f < 2 else None
                    x = w[f][j]
                    new = A[f * groups + j] + spatial(x, u, v, eu, ev, visc, everything)
                    up = down[j - 1][f] if j > 0 else roll_lanes(down[groups - 1][f], BLOCK)
                    new = new + (down[j][f] - up)
                    if f == 2:
                        new = new - (drag * x + cor * w[3][j])
                    if f == 3:
                        new = new - (drag * x - cor * w[2][j])
                    B[f * groups + j] = new
                    J[f * groups + j] = jnp.where(place < 10, new, roll_lanes(new, -12))

        wet_top = 2 * levels

        def begin(A):
            wet = ST[wet_top + levels - 1]
            w = [wet * A[f, levels] for f in range(fields)]
            nothing = jnp.zeros((wide, cols), jnp.float32)
            return (nothing, nothing, *w, nothing, nothing, nothing, nothing)

        def level(A, k, carry, part, write):
            cu, cv, *rest = carry
            w, g = rest[:4], rest[4:]
            kf = jnp.asarray(k, jnp.int32).astype(jnp.float32)
            first = kf + jnp.where(k == 0, 1000.0, 0.0)
            depth, visc, cor = ST[misc + 1], ST[misc], SC[2][part]
            wet_up = ST[wet_top + jnp.where(k == 0, 0, k - 1)]
            mix = jnp.where(depth > first, mixing_rate, 0.0)
            drag = jnp.where(depth[part] == kf + 1.0, drag_rate, 0.0)
            u, v = ST[k], ST[levels + k]
            cu, cv = cu + w[2], cv + w[3]
            w_up = [wet_up * A[f, k] for f in range(fields)]
            g_up = [mix * (w[f] - w_up[f]) for f in range(fields)]
            for f in range(fields):
                h = (half_t, half_s, 0.0, 0.0)[f]
                eu = h * cu if f < 2 else None
                ev = h * cv if f < 2 else None
                new = A[f, k + 1][part] + spatial(w[f], u, v, eu, ev, visc, part)
                new = new + (g[f][part] - g_up[f][part])
                if f == 2:
                    new = new - (drag * w[2][part] + cor * w[3][part])
                if f == 3:
                    new = new - (drag * w[3][part] - cor * w[2][part])
                write(f, k, new)
            return (cu, cv, *w_up, *g_up)

        def sweep(A, carry, first, last, part, write):
            def body(i, carry):
                for j in range(UNROLL):
                    carry = level(A, first - i * UNROLL - j, carry, part, write)
                return carry

            return lax.fori_loop(0, (first - last + 1) // UNROLL, body, carry)

        def fixed(f, k, part, edge, new):
            b = k // groups
            x = pltpu.roll(J[f * groups + lax.rem(k, groups), part, :], 118 - BLOCK * b, 1)
            return jnp.where(edge[part], x, new)

        def store_flux(A, step):
            for f in range(fields):
                at_row = (step * fields + f) * rows
                H[at_row : at_row + rows] = A[f, 1, own, :] * ST[wet_top, own, :]

        def surface(A, S, B, R, i):
            for f in range(fields):
                R[f * groups] = R[f * groups] + SG[f] * (FS[i * fields + f] - S[f * groups])
                gain = ST[wet_top] * ST[misc + 2 + f]
                B[f, 1] = B[f, 1] + gain * (F[i * fields + f] - A[f, 1])

        store_flux(A0, 2)
        strip_step(SP, SN)

        def write1(f, k, new):
            A1[f, k + 1] = fixed(f, k, everything, edge2, new)

        sweep(A0, begin(A0), levels - 1, 0, everything, write1)

        all_of(SB1, RB1, a2a_recv.at[0]).wait()
        for b in range(n_lat):
            parts = []
            for q in range(q_share):
                parts.append(RB1[pl.ds(b * n_lon * q_pad + q, n_lon, stride=q_pad), :])
            t = jnp.concatenate(parts, axis=0).T
            G[pl.ds(b, lines, stride=n_lat), :] = t[:lines]
        for i, step in ((0, 2), (1, 1)):
            for f in range(fields):
                at_row = (step * fields + f) * rows
                F[i * fields + f, own, :] = G[at_row : at_row + rows]
        packed = [pack([F[i * fields + f, own, :] for f in range(4)]) for i in range(2)]
        FE[0] = message(packed, 4)
        FW[0] = message(packed, 10)
        both, up, down = strip_copies(FE, FW, FRE, FRW, f_send, f_recv)
        up = up + [remote(F.at[:, pl.ds(rows, PAD), :], F.at[:, low, :], f_send, f_recv, 6, lat + 1, lon)]
        down = down + [remote(F.at[:, pl.ds(PAD, PAD), :], F.at[:, high, :], f_send, f_recv, 7, lat - 1, lon)]
        f_halo = (both, up, down)
        start(f_halo)

        def write2(f, k, new):
            A0[f, k + 1] = new

        carry = sweep(A1, begin(A1), levels - 1, groups, everything, write2)

        finish_recv(f_halo)
        for i in range(2):
            x = lay(pack([F[i * fields + f] for f in range(4)]))
            x = jnp.where((place >= 10) & (place < 16), roll_lanes(FRE[0], 10 - 8 * i), x)
            x = jnp.where((place >= 16) & (place < 22), roll_lanes(FRW[0], 16 - 8 * i), x)
            for f in range(fields):
                FS[i * fields + f] = roll_lanes(x, -BLOCK * f)
        surface(A0, SP, A1, SN, 0)
        store_flux(A1, 1)
        strip_step(SN, SP)
        sweep(A1, carry, groups - 1, 0, everything, write2)
        for f in range(fields):
            A0[f, 1] = fixed(f, 0, everything, edge2, A0[f, 1])
        surface(A1, SN, A0, SP, 1)
        store_flux(A0, 0)

        for b in range(n_lat):
            t = transposed(H[pl.ds(b, lines, stride=n_lat), :])
            for q in range(q_share):
                SB2[pl.ds(b * n_lon * q_pad + q, n_lon, stride=q_pad), :] = t[q * n_lon : (q + 1) * n_lon]
        exchange(SB2, RB2, 1)

        strip_step(SP, SN)

        def write3(f, k, new):
            out[f, k] = fixed(f, k, own, edge4, new)

        sweep(A0, begin(A0), levels - 1, 0, own, write3)
        for f in range(fields):
            gain = ST[wet_top, own, :] * ST[misc + 2 + f, own, :]
            out[f, 0] = out[f, 0] + gain * (G[f * rows : (f + 1) * rows] - A0[f, 1, own, :])

        all_of(SB2, RB2, a2a_recv.at[1]).wait()
        for b in range(n_lat):
            starts = [(b * n_lon + a) * q_pad for a in range(n_lon)]
            x = jnp.concatenate([RB2[i : i + q_share, :] for i in starts], axis=0)
            t = x.T[:lines]
            flux[:, :, b * s_share : (b + 1) * s_share, :] = t.reshape(window, fields, s_share, cols)
        finish_send(halo)
        finish_send(side)
        finish_send(f_halo)
        all_of(SB1, RB1, a2a_send.at[0]).wait()
        all_of(SB2, RB2, a2a_send.at[1]).wait()

    return kernel


def local(
    final_adjoint, drift_u, drift_v, wet_mask, bottom_level, viscosity, bulk_rate, atmos_adjoint
):
    fields, levels, rows, cols = final_adjoint.shape
    window = atmos_adjoint.shape[0]
    n_lat, n_lon = lax.axis_size("lat"), lax.axis_size("lon")
    n = n_lat * n_lon
    wide = rows + 2 * PAD
    q_share = cols // n_lon
    q_pad = -(-q_share // 8) * 8
    groups = levels // 4
    strips = (fields + 3) * groups + 2
    messages = -(-strips // 4)

    def buf(*shape):
        return pltpu.VMEM(shape, jnp.float32)

    kernel = make_kernel(n_lat, n_lon, fields, levels, rows, cols, window, q_share, q_pad)
    f32 = jnp.float32
    anywhere = pl.BlockSpec(memory_space=pl.ANY)
    return pl.pallas_call(
        kernel,
        out_shape=(
            pltpu.VMEM(final_adjoint.shape, f32),
            pltpu.VMEM(atmos_adjoint.shape, f32),
        ),
        in_specs=[anywhere] * 8,
        out_specs=(pl.BlockSpec(memory_space=pltpu.VMEM),) * 2,
        scratch_shapes=[
            buf(window, fields, rows, cols),
            buf(fields, levels + 1, wide, cols), buf(fields, levels + 1, wide, cols),
            buf(3 * levels + 2 + fields, wide, cols),
            pltpu.VMEM((levels, wide, cols), jnp.int32), pltpu.VMEM((wide, cols), jnp.int32),
            buf(strips, wide, cols), buf(fields * groups, wide, cols),
            buf(3, wide, cols), buf(fields, wide, cols), buf(fields * groups, wide, cols),
            buf(messages, rows, cols), buf(messages, rows, cols),
            buf(messages, wide, cols), buf(messages, wide, cols),
            buf(2 * fields, wide, cols), buf(2 * fields, wide, cols),
            buf(1, rows, cols), buf(1, rows, cols), buf(1, wide, cols), buf(1, wide, cols),
            buf(window * fields * rows, cols), buf(window * fields * rows, cols),
            buf(n * q_pad, cols), buf(n * q_pad, cols), buf(n * q_pad, cols), buf(n * q_pad, cols),
            pltpu.SemaphoreType.DMA((14,)), pltpu.SemaphoreType.DMA((14,)),
            pltpu.SemaphoreType.DMA((6,)), pltpu.SemaphoreType.DMA((6,)),
            pltpu.SemaphoreType.DMA((8,)), pltpu.SemaphoreType.DMA((8,)),
            pltpu.SemaphoreType.DMA((2,)), pltpu.SemaphoreType.DMA((2,)), pltpu.SemaphoreType.DMA((8,)),
        ],
        compiler_params=pltpu.CompilerParams(
            collective_id=0, has_side_effects=True, vmem_limit_bytes=60 * 1024 * 1024
        ),
    )(final_adjoint, drift_u, drift_v, wet_mask, bottom_level, viscosity, bulk_rate, atmos_adjoint)


def solution(mesh):
    in_specs = (
        P(None, None, "lat", "lon"),
        P(None, "lat", "lon"),
        P(None, "lat", "lon"),
        P(None, "lat", "lon"),
        P("lat", "lon"),
        P("lat", "lon"),
        P(None, "lat", "lon"),
        P(None, None, "lat", "lon"),
    )
    out_specs = (P(None, None, "lat", "lon"), P(None, None, "lat", "lon"))
    return jax.shard_map(local, mesh=mesh, in_specs=in_specs, out_specs=out_specs, check_vma=False)
```

```python
import math

import jax
import jax.numpy as jnp
from jax import lax
from jax.experimental import pallas as pl
from jax.experimental.pallas import tpu as pltpu
from jax.sharding import PartitionSpec as P

lap_weight = 0.04
mixing_rate = 0.15
drag_rate = 0.2
expansion = 0.2
contraction = 0.15
pressure_weight = 0.1
coriolis_scale = 0.2

MESH = pl.DeviceIdType.MESH
PAD = 8
BLOCK = 32
UNROLL = 3


def roll_lanes(x, shift):
    shift = shift % x.shape[-1]
    return pltpu.roll(x, shift, x.ndim - 1) if shift else x


def east(x):
    return roll_lanes(x, -1)


def west(x):
    return roll_lanes(x, 1)


def north(x):
    return pltpu.roll(x, x.shape[0] - 1, 0)


def south(x):
    return pltpu.roll(x, 1, 0)


def make_kernel(n_lat, n_lon, fields, levels, rows, cols, window, q_share):
    n = n_lat * n_lon
    wide = rows + 2 * PAD
    total_rows = rows * n_lat
    s_share = rows // n_lat
    lines = fields * s_share
    per = BLOCK // n_lon
    misc = 3 * levels
    groups = levels // 4
    strips = (fields + 3) * groups + 2
    messages = -(-strips // 4)

    def kernel(
        fa, du, dv, wm, bl, vi, br, at_hbm,
        out, flux,
        at, A0, A1, ST, WI, BI, SP, SN, SC, SG, J, ME, MW, RE, RW, F, FS, FE, FW, FRE, FRW,
        Y, FL, SB, RB,
        halo_send, halo_recv, side_send, side_recv, f_send, f_recv, a2a_send, a2a_recv, in_sem,
    ):
        lat = lax.axis_index("lat")
        lon = lax.axis_index("lon")
        me = lat * n_lon + lon
        eastward = lax.rem(lon + 1, n_lon)
        westward = lax.rem(lon + n_lon - 1, n_lon)

        mid_rows = pl.ds(PAD, rows)
        inner = pl.ds(1, levels)
        loads = [
            pltpu.make_async_copy(src, dst, in_sem.at[i])
            for i, (src, dst) in enumerate([
                (at_hbm, at),
                (fa, A0.at[:, inner, mid_rows, :]),
                (du, ST.at[pl.ds(0, levels), mid_rows, :]),
                (dv, ST.at[pl.ds(levels, levels), mid_rows, :]),
                (wm, WI.at[:, mid_rows, :]),
                (bl, BI.at[mid_rows, :]),
                (vi, ST.at[misc, mid_rows, :]),
                (br, ST.at[pl.ds(misc + 2, fields), mid_rows, :]),
            ])
        ]
        for c in loads:
            c.start()

        barrier = pltpu.get_barrier_semaphore()

        @pl.loop(1, n)
        def _(k):
            other = lax.rem(me + k, n)
            pl.semaphore_signal(
                barrier, inc=1, device_id={"lat": other // n_lon, "lon": lax.rem(other, n_lon)},
                device_id_type=MESH,
            )

        lane = lax.broadcasted_iota(jnp.int32, (wide, cols), 1)
        place = lane & (BLOCK - 1)
        block = lane >> (BLOCK.bit_length() - 1)
        row = lax.broadcasted_iota(jnp.int32, (wide, cols), 0) + lat * rows - PAD
        own = slice(PAD, PAD + rows)
        low = slice(0, PAD)
        high = slice(PAD + rows, wide)
        everything = slice(0, wide)

        def pack(planes):
            height = planes[0].shape[0]
            b = block[:height]
            x = roll_lanes(planes[0], -118)
            for f in range(1, 4):
                x = jnp.where(b == f, roll_lanes(planes[f], BLOCK * f - 118), x)
            return x

        def message(packed, base):
            height = packed[0].shape[0]
            p = place[:height] // 8
            x = roll_lanes(packed[0], -base)
            for j in range(1, len(packed)):
                x = jnp.where(p == j, roll_lanes(packed[j], 8 * j - base), x)
            return x

        def lay(packed):
            return jnp.where(place[: packed.shape[0]] < 10, packed, roll_lanes(packed, 12))

        for ref in (A0, A1):
            ref[:, 0:1] = jnp.zeros((fields, 1, wide, cols), jnp.float32)

        def clear(part):
            A0[:, 1 : levels + 1, part, :] = jnp.zeros((fields, levels, PAD, cols), jnp.float32)
            ST[:, part, :] = jnp.zeros((misc + 2 + fields, PAD, cols), jnp.float32)
            WI[:, part, :] = jnp.zeros((levels, PAD, cols), jnp.int32)
            BI[part, :] = jnp.zeros((PAD, cols), jnp.int32)
            F[:, part, :] = jnp.zeros((2 * fields, PAD, cols), jnp.float32)
            for ref in (RE, RW, FRE, FRW):
                ref[:, part, :] = jnp.zeros((ref.shape[0], PAD, cols), jnp.float32)

        @pl.when(lat == 0)
        def _():
            clear(low)

        @pl.when(lat == n_lat - 1)
        def _():
            clear(high)

        angle = math.pi * (row.astype(jnp.float32) + 0.5) / total_rows - math.pi / 2
        SC[2] = coriolis_scale * jnp.sin(angle)

        def remote(src, dst, send, recv, i, to_lat, to_lon):
            return pltpu.make_async_remote_copy(
                src_ref=src, dst_ref=dst, send_sem=send.at[i], recv_sem=recv.at[i],
                device_id={"lat": to_lat, "lon": to_lon}, device_id_type=MESH,
            )

        def strip_copies(to_e, to_w, from_e, from_w, send, recv):
            both = [
                remote(to_e, from_w.at[:, mid_rows, :], send, recv, 0, lat, eastward),
                remote(to_w, from_e.at[:, mid_rows, :], send, recv, 1, lat, westward),
            ]
            top, bottom = pl.ds(rows - PAD, PAD), pl.ds(0, PAD)
            up = [
                remote(to_e.at[:, top, :], from_w.at[:, low, :], send, recv, 2, lat + 1, eastward),
                remote(to_w.at[:, top, :], from_e.at[:, low, :], send, recv, 3, lat + 1, westward),
            ]
            down = [
                remote(to_e.at[:, bottom, :], from_w.at[:, high, :], send, recv, 4, lat - 1, eastward),
                remote(to_w.at[:, bottom, :], from_e.at[:, high, :], send, recv, 5, lat - 1, westward),
            ]
            return both, up, down

        def start(copies):
            both, up, down = copies
            for c in both:
                c.start()

            @pl.when(lat < n_lat - 1)
            def _():
                for c in up:
                    c.start()

            @pl.when(lat > 0)
            def _():
                for c in down:
                    c.start()

        def finish_recv(copies):
            both, up, down = copies
            for c in both:
                c.wait_recv()

            @pl.when(lat > 0)
            def _():
                for c in up:
                    c.wait_recv()

            @pl.when(lat < n_lat - 1)
            def _():
                for c in down:
                    c.wait_recv()

        def finish_send(copies):
            both, up, down = copies
            for c in both:
                c.wait_send()

            @pl.when(lat < n_lat - 1)
            def _():
                for c in up:
                    c.wait_send()

            @pl.when(lat > 0)
            def _():
                for c in down:
                    c.wait_send()

        def rims(to, start_row, i, to_lat):
            src, dst = pl.ds(start_row, PAD), to
            return [
                remote(fa.at[:, :, src, :], A0.at[:, inner, dst, :], halo_send, halo_recv, i, to_lat, lon),
                remote(du.at[:, src, :], ST.at[pl.ds(0, levels), dst, :], halo_send, halo_recv, i + 1, to_lat, lon),
                remote(dv.at[:, src, :], ST.at[pl.ds(levels, levels), dst, :], halo_send, halo_recv, i + 2, to_lat, lon),
                remote(wm.at[:, src, :], WI.at[:, dst, :], halo_send, halo_recv, i + 3, to_lat, lon),
                remote(bl.at[src, :], BI.at[dst, :], halo_send, halo_recv, i + 4, to_lat, lon),
                remote(vi.at[src, :], ST.at[misc, dst, :], halo_send, halo_recv, i + 5, to_lat, lon),
                remote(br.at[:, src, :], ST.at[pl.ds(misc + 2, fields), dst, :], halo_send, halo_recv, i + 6, to_lat, lon),
            ]

        halo = ([], rims(low, rows - PAD, 0, lat + 1), rims(high, 0, 7, lat - 1))
        side = strip_copies(ME, MW, RE, RW, side_send, side_recv)

        pl.semaphore_wait(barrier, n - 1)
        start(halo)

        def convert(part):
            for k in range(levels):
                ST[k, part, :] = 0.5 * ST[k, part, :]
                ST[levels + k, part, :] = 0.5 * ST[levels + k, part, :]
                ST[2 * levels + k, part, :] = WI[k, part, :].astype(jnp.float32)
            ST[misc + 1, part, :] = BI[part, :].astype(jnp.float32)

        def sources(i, part):
            if i < fields * groups:
                f, j = divmod(i, groups)
                return [A0[f, b * groups + j + 1, part, :] for b in range(4)]
            if i < (fields + 3) * groups:
                kind, j = divmod(i - fields * groups, groups)
                return [ST[kind * levels + b * groups + j, part, :] for b in range(4)]
            if i == (fields + 3) * groups:
                v, d = ST[misc, part, :], ST[misc + 1, part, :]
                return [v, d, v, d]
            return [ST[misc + 2 + f, part, :] for f in range(4)]

        for c in loads[1:]:
            c.wait()
        convert(own)
        for m in range(messages):
            ids = range(4 * m, min(4 * m + 4, strips))
            packed = [pack(sources(i, own)) for i in ids]
            ME[m] = message(packed, 4)
            MW[m] = message(packed, 10)
            for i, x in zip(ids, packed):
                SP[i, own, :] = lay(x)
        start(side)

        def across(x):
            return jnp.concatenate([x] * 4, axis=0).T

        def by_block(t, which):
            height = t.shape[0] // 4
            x = t[:height]
            for r in range(1, 4):
                x = jnp.where(which == r, t[r * height : (r + 1) * height], x)
            return x

        part_of = (lane[:lines] & (q_share - 1)) // per
        part_block = block[:lines]

        def pack_forcing(step, e, i):
            for b in range(n_lat):
                x = at[step, :, b * s_share : (b + 1) * s_share, :].reshape(lines, cols)
                Y[b] = across(x)
                for p in range(per):
                    x = Y[b, pl.ds(p, n_lon, stride=q_share), :]
                    for r in range(1, 4):
                        x = jnp.where(block[:n_lon] == r, Y[b, pl.ds(per * r + p, n_lon, stride=q_share), :], x)
                    SB[e, pl.ds(b * n_lon * 8 + i * per + p, n_lon, stride=8), :] = x

        def unpack_forcing(e, i, to):
            for b in range(n_lat):
                x = jnp.concatenate(
                    [RB[e, pl.ds(b * n_lon * 8 + i * per + p, n_lon, stride=8), :] for p in range(per)], axis=0
                )
                to[pl.ds(b, lines, stride=n_lat), :] = by_block(across(x), part_block)

        def pack_flux(e, i):
            for b in range(n_lat):
                x = by_block(across(FL[pl.ds(b, lines, stride=n_lat), :]), block[:BLOCK])
                for p in range(per):
                    at_row = b * n_lon * 8 + i * per + p
                    SB[e, pl.ds(at_row, n_lon, stride=8), :] = x[p * n_lon : (p + 1) * n_lon]

        def unpack_flux(e, i, step):
            for b in range(n_lat):
                for p in range(per):
                    x = RB[e, pl.ds(b * n_lon * 8 + i * per + p, n_lon, stride=8), :]
                    for r in range(4):
                        Y[b, pl.ds(per * r + p, n_lon, stride=q_share), :] = x
                x = by_block(Y[b].T, part_of)
                flux[step, :, b * s_share : (b + 1) * s_share, :] = x.reshape(fields, s_share, cols)

        def place_of(device, size):
            return pl.ds(pl.multiple_of(device * 8, 8), size)

        def exchange(e, size):
            def send(la, lo):
                pltpu.make_async_remote_copy(
                    src_ref=SB.at[e, place_of(la * n_lon + lo, size)], dst_ref=RB.at[e, place_of(me, size)],
                    send_sem=a2a_send.at[e], recv_sem=a2a_recv.at[e],
                    device_id={"lat": la, "lon": lo}, device_id_type=MESH,
                ).start()

            for dl in range(n_lat):
                la = lax.rem(lat + dl, n_lat)
                least = 1 if dl == 0 else 0
                if n_lon <= 8:
                    for dn in range(least, n_lon):
                        send(la, lax.rem(lon + dn, n_lon))
                else:
                    @pl.loop(least, n_lon)
                    def _(dn):
                        send(la, lax.rem(lon + dn, n_lon))

            RB[e, place_of(me, 8), :] = SB[e, place_of(me, 8), :]

        def all_of(e, size, sem):
            some = pl.ds(0, (n - 1) * size)
            pltpu.make_async_copy(SB.at[e, some], RB.at[e, some], sem.at[e]).wait()

        loads[0].wait()
        pack_forcing(2, 0, 0)
        pack_forcing(1, 0, 1)
        exchange(0, 2 * per)

        def store_flux(A):
            for f in range(fields):
                FL[f * rows : (f + 1) * rows] = A[f, 1, own, :] * ST[2 * levels, own, :]

        pack_forcing(0, 1, 0)
        store_flux(A0)
        pack_flux(1, 1)

        finish_recv(halo)
        for part in (low, high):
            convert(part)
            for i in range(strips):
                SP[i, part, :] = lay(pack(sources(i, part)))

        finish_recv(side)
        between = (place >= 10) & (place < 22)
        half = lane & 15
        for m in range(messages):
            from_e, from_w = RE[m], roll_lanes(RW[m], 6)
            even = jnp.where(half < 6, from_e, from_w)
            odd = jnp.where((half >= 8) & (half < 14), from_e, from_w)
            for p in range(min(4, strips - 4 * m)):
                x = roll_lanes((even, odd)[p % 2], 10 - 8 * p)
                SP[4 * m + p] = jnp.where(between, x, SP[4 * m + p])

        strip_u, strip_v, strip_wet = [(fields + i) * groups for i in range(3)]
        x = SP[(fields + 3) * groups]
        SC[0] = jnp.where((block & 1) == 0, x, roll_lanes(x, BLOCK))
        SC[1] = jnp.where((block & 1) == 1, x, roll_lanes(x, -BLOCK)) - (block * groups).astype(jnp.float32)
        x = SP[(fields + 3) * groups + 1]
        for f in range(fields):
            SG[f] = jnp.where(block == 0, SP[strip_wet] * roll_lanes(x, -BLOCK * f), 0.0)

        half_t = 0.5 * pressure_weight * expansion
        half_s = -0.5 * pressure_weight * contraction
        edge2 = (lane < 2) | (lane >= cols - 2)
        edge4 = (lane < 4) | (lane >= cols - 4)
        keep_low = jnp.where(lat > 0, 1.0, 0.0)
        keep_high = jnp.where(lat < n_lat - 1, 1.0, 0.0)

        def masked(x):
            return jnp.concatenate([x[low] * keep_low, x[own], x[high] * keep_high], axis=0)

        def spatial(w, u, v, extra_u, extra_v, visc, part):
            y = visc * w
            inner_lap = (north(y) + south(y)) - 4.0 * y
            z = lap_weight * w - masked(inner_lap)
            along, across = u * w, v * w
            if extra_u is not None:
                along, across = along + extra_u, across + extra_v
            vertical = north(z + across) + south(z - across)
            z, y, along = z[part], y[part], along[part]
            t = z - inner_lap[part]
            flat = (east(t + along) + west(t - along)) - (roll_lanes(y, -2) + roll_lanes(y, 2))
            return (flat + vertical[part]) - (4.0 * z + 2.0 * y)

        def strip_step(A, B):
            depth, visc, cor = SC[1], SC[0], SC[2]
            w = [[SP[strip_wet + j] * A[f * groups + j] for j in range(groups)] for f in range(fields)]
            sums = []
            for f in (2, 3):
                c = [w[f][groups - 1]]
                for j in range(groups - 2, -1, -1):
                    c.insert(0, c[0] + w[f][j])
                later = 0.0
                for b in range(1, 4):
                    later = later + jnp.where(block < 4 - b, roll_lanes(c[0], -BLOCK * b), 0.0)
                sums.append([x + later for x in c])
            down = []
            for j in range(groups):
                mix = jnp.where(depth > j + 1.0, mixing_rate, 0.0)
                down.append([
                    mix * ((w[f][j + 1] if j < groups - 1 else roll_lanes(w[f][0], -BLOCK)) - w[f][j])
                    for f in range(fields)
                ])
            for j in range(groups):
                drag = jnp.where(depth == j + 1.0, drag_rate, 0.0)
                u, v = SP[strip_u + j], SP[strip_v + j]
                for f in range(fields):
                    h = (half_t, half_s, 0.0, 0.0)[f]
                    eu = h * sums[0][j] if f < 2 else None
                    ev = h * sums[1][j] if f < 2 else None
                    x = w[f][j]
                    new = A[f * groups + j] + spatial(x, u, v, eu, ev, visc, everything)
                    up = down[j - 1][f] if j > 0 else roll_lanes(down[groups - 1][f], BLOCK)
                    new = new + (down[j][f] - up)
                    if f == 2:
                        new = new - (drag * x + cor * w[3][j])
                    if f == 3:
                        new = new - (drag * x - cor * w[2][j])
                    B[f * groups + j] = new
                    J[f * groups + j] = jnp.where(place < 10, new, roll_lanes(new, -12))

        wet_top = 2 * levels

        def begin(A):
            wet = ST[wet_top + levels - 1]
            w = [wet * A[f, levels] for f in range(fields)]
            nothing = jnp.zeros((wide, cols), jnp.float32)
            return (nothing, nothing, *w, nothing, nothing, nothing, nothing)

        def level(A, k, carry, part, write):
            cu, cv, *rest = carry
            w, g = rest[:4], rest[4:]
            kf = jnp.asarray(k, jnp.int32).astype(jnp.float32)
            first = kf + jnp.where(k == 0, 1000.0, 0.0)
            depth, visc, cor = ST[misc + 1], ST[misc], SC[2][part]
            wet_up = ST[wet_top + jnp.where(k == 0, 0, k - 1)]
            mix = jnp.where(depth > first, mixing_rate, 0.0)
            drag = jnp.where(depth[part] == kf + 1.0, drag_rate, 0.0)
            u, v = ST[k], ST[levels + k]
            cu, cv = cu + w[2], cv + w[3]
            w_up = [wet_up * A[f, k] for f in range(fields)]
            g_up = [mix * (w[f] - w_up[f]) for f in range(fields)]
            for f in range(fields):
                h = (half_t, half_s, 0.0, 0.0)[f]
                eu = h * cu if f < 2 else None
                ev = h * cv if f < 2 else None
                new = A[f, k + 1][part] + spatial(w[f], u, v, eu, ev, visc, part)
                new = new + (g[f][part] - g_up[f][part])
                if f == 2:
                    new = new - (drag * w[2][part] + cor * w[3][part])
                if f == 3:
                    new = new - (drag * w[3][part] - cor * w[2][part])
                write(f, k, new)
            return (cu, cv, *w_up, *g_up)

        def sweep(A, carry, first, last, part, write):
            def body(i, carry):
                for j in range(UNROLL):
                    carry = level(A, first - i * UNROLL - j, carry, part, write)
                return carry

            return lax.fori_loop(0, (first - last + 1) // UNROLL, body, carry)

        def fixed(f, k, part, edge, new):
            b = k // groups
            x = pltpu.roll(J[f * groups + lax.rem(k, groups), part, :], 118 - BLOCK * b, 1)
            return jnp.where(edge[part], x, new)

        def surface(A, S, B, R, i):
            for f in range(fields):
                R[f * groups] = R[f * groups] + SG[f] * (FS[i * fields + f] - S[f * groups])
                gain = ST[wet_top] * ST[misc + 2 + f]
                B[f, 1] = B[f, 1] + gain * (F[i * fields + f] - A[f, 1])

        all_of(0, 2 * per, a2a_recv)
        for i in range(2):
            unpack_forcing(0, i, FL)
            for f in range(fields):
                F[i * fields + f, own, :] = FL[f * rows : (f + 1) * rows]
        packed = [pack([F[i * fields + f, own, :] for f in range(4)]) for i in range(2)]
        FE[0] = message(packed, 4)
        FW[0] = message(packed, 10)
        both, up, down = strip_copies(FE, FW, FRE, FRW, f_send, f_recv)
        up = up + [remote(F.at[:, pl.ds(rows, PAD), :], F.at[:, low, :], f_send, f_recv, 6, lat + 1, lon)]
        down = down + [remote(F.at[:, pl.ds(PAD, PAD), :], F.at[:, high, :], f_send, f_recv, 7, lat - 1, lon)]
        f_halo = (both, up, down)
        start(f_halo)
        strip_step(SP, SN)

        def write1(f, k, new):
            A1[f, k + 1] = fixed(f, k, everything, edge2, new)

        sweep(A0, begin(A0), levels - 1, 0, everything, write1)


        exchange(1, 2 * per)

        def write2(f, k, new):
            A0[f, k + 1] = new

        carry = sweep(A1, begin(A1), levels - 1, groups, everything, write2)

        finish_recv(f_halo)
        for i in range(2):
            x = lay(pack([F[i * fields + f] for f in range(4)]))
            x = jnp.where((place >= 10) & (place < 16), roll_lanes(FRE[0], 10 - 8 * i), x)
            x = jnp.where((place >= 16) & (place < 22), roll_lanes(FRW[0], 16 - 8 * i), x)
            for f in range(fields):
                FS[i * fields + f] = roll_lanes(x, -BLOCK * f)
        surface(A0, SP, A1, SN, 0)
        store_flux(A1)
        pack_flux(2, 0)
        exchange(2, per)
        strip_step(SN, SP)
        sweep(A1, carry, groups - 1, 0, everything, write2)
        for f in range(fields):
            A0[f, 1] = fixed(f, 0, everything, edge2, A0[f, 1])
        surface(A1, SN, A0, SP, 1)
        store_flux(A0)
        pack_flux(3, 0)
        exchange(3, per)

        strip_step(SP, SN)

        def write3(f, k, new):
            out[f, k] = fixed(f, k, own, edge4, new)

        sweep(A0, begin(A0), levels - 1, 0, own, write3)
        all_of(1, 2 * per, a2a_recv)
        unpack_forcing(1, 0, FL)
        for f in range(fields):
            gain = ST[wet_top, own, :] * ST[misc + 2 + f, own, :]
            out[f, 0] = out[f, 0] + gain * (FL[f * rows : (f + 1) * rows] - A0[f, 1, own, :])

        unpack_flux(1, 1, 2)
        all_of(2, per, a2a_recv)
        unpack_flux(2, 0, 1)
        all_of(3, per, a2a_recv)
        unpack_flux(3, 0, 0)
        finish_send(halo)
        finish_send(side)
        finish_send(f_halo)
        for e in range(4):
            all_of(e, (2 * per, 2 * per, per, per)[e], a2a_send)

    return kernel


def local(
    final_adjoint, drift_u, drift_v, wet_mask, bottom_level, viscosity, bulk_rate, atmos_adjoint
):
    fields, levels, rows, cols = final_adjoint.shape
    window = atmos_adjoint.shape[0]
    n_lat, n_lon = lax.axis_size("lat"), lax.axis_size("lon")
    n = n_lat * n_lon
    wide = rows + 2 * PAD
    q_share = cols // n_lon
    groups = levels // 4
    strips = (fields + 3) * groups + 2
    messages = -(-strips // 4)

    def buf(*shape):
        return pltpu.VMEM(shape, jnp.float32)

    kernel = make_kernel(n_lat, n_lon, fields, levels, rows, cols, window, q_share)
    f32 = jnp.float32
    anywhere = pl.BlockSpec(memory_space=pl.ANY)
    return pl.pallas_call(
        kernel,
        out_shape=(
            pltpu.VMEM(final_adjoint.shape, f32),
            pltpu.VMEM(atmos_adjoint.shape, f32),
        ),
        in_specs=[anywhere] * 8,
        out_specs=(pl.BlockSpec(memory_space=pltpu.VMEM),) * 2,
        scratch_shapes=[
            buf(window, fields, rows, cols),
            buf(fields, levels + 1, wide, cols), buf(fields, levels + 1, wide, cols),
            buf(3 * levels + 2 + fields, wide, cols),
            pltpu.VMEM((levels, wide, cols), jnp.int32), pltpu.VMEM((wide, cols), jnp.int32),
            buf(strips, wide, cols), buf(fields * groups, wide, cols),
            buf(3, wide, cols), buf(fields, wide, cols), buf(fields * groups, wide, cols),
            buf(messages, rows, cols), buf(messages, rows, cols),
            buf(messages, wide, cols), buf(messages, wide, cols),
            buf(2 * fields, wide, cols), buf(2 * fields, wide, cols),
            buf(1, rows, cols), buf(1, rows, cols), buf(1, wide, cols), buf(1, wide, cols),
            buf(n_lat, cols, cols), buf(fields * rows, cols), buf(4, n * 8, cols), buf(4, n * 8, cols),
            pltpu.SemaphoreType.DMA((14,)), pltpu.SemaphoreType.DMA((14,)),
            pltpu.SemaphoreType.DMA((6,)), pltpu.SemaphoreType.DMA((6,)),
            pltpu.SemaphoreType.DMA((8,)), pltpu.SemaphoreType.DMA((8,)),
            pltpu.SemaphoreType.DMA((4,)), pltpu.SemaphoreType.DMA((4,)), pltpu.SemaphoreType.DMA((8,)),
        ],
        compiler_params=pltpu.CompilerParams(
            collective_id=0, has_side_effects=True, vmem_limit_bytes=60 * 1024 * 1024
        ),
    )(final_adjoint, drift_u, drift_v, wet_mask, bottom_level, viscosity, bulk_rate, atmos_adjoint)


def solution(mesh):
    in_specs = (
        P(None, None, "lat", "lon"),
        P(None, "lat", "lon"),
        P(None, "lat", "lon"),
        P(None, "lat", "lon"),
        P("lat", "lon"),
        P("lat", "lon"),
        P(None, "lat", "lon"),
        P(None, None, "lat", "lon"),
    )
    out_specs = (P(None, None, "lat", "lon"), P(None, None, "lat", "lon"))
    return jax.shard_map(local, mesh=mesh, in_specs=in_specs, out_specs=out_specs, check_vma=False)
```

```python
import math

import jax
import jax.numpy as jnp
from jax import lax
from jax.experimental import pallas as pl
from jax.experimental.pallas import tpu as pltpu
from jax.sharding import PartitionSpec as P

lap_weight = 0.04
mixing_rate = 0.15
drag_rate = 0.2
expansion = 0.2
contraction = 0.15
pressure_weight = 0.1
coriolis_scale = 0.2

MESH = pl.DeviceIdType.MESH
PAD = 8
RIM = 6
BLOCK = 32
UNROLL = 3


def roll_lanes(x, shift):
    shift = shift % x.shape[-1]
    return pltpu.roll(x, shift, x.ndim - 1) if shift else x


def east(x):
    return roll_lanes(x, -1)


def west(x):
    return roll_lanes(x, 1)


def north(x):
    return pltpu.roll(x, x.shape[0] - 1, 0)


def south(x):
    return pltpu.roll(x, 1, 0)


def make_kernel(n_lat, n_lon, fields, levels, rows, cols, window, q_share):
    n = n_lat * n_lon
    wide = rows + 2 * PAD
    total_rows = rows * n_lat
    s_share = rows // n_lat
    lines = fields * s_share
    per = BLOCK // n_lon
    misc = 3 * levels
    groups = levels // 4
    strips = (fields + 3) * groups + 2
    messages = -(-strips // 4)

    def kernel(
        fa, du, dv, wm, bl, vi, br, at_hbm,
        out, flux,
        at, A0, A1, ST, WI, BI, SP, SN, SC, SG, J, ME, MW, RE, RW, F, FS, FE, FW, FRE, FRW,
        Y, FL, SB, RB,
        halo_send, halo_recv, side_send, side_recv, f_send, f_recv, a2a_send, a2a_recv, in_sem,
    ):
        lat = lax.axis_index("lat")
        lon = lax.axis_index("lon")
        me = lat * n_lon + lon
        eastward = lax.rem(lon + 1, n_lon)
        westward = lax.rem(lon + n_lon - 1, n_lon)

        mid_rows = pl.ds(PAD, rows)
        inner = pl.ds(1, levels)
        loads = [
            pltpu.make_async_copy(src, dst, in_sem.at[min(i, 2)])
            for i, (src, dst) in enumerate([
                (at_hbm, at),
                (fa, A0.at[:, inner, mid_rows, :]),
                (du, ST.at[pl.ds(0, levels), mid_rows, :]),
                (dv, ST.at[pl.ds(levels, levels), mid_rows, :]),
                (wm, WI.at[:, mid_rows, :]),
                (bl, BI.at[mid_rows, :]),
                (vi, ST.at[misc, mid_rows, :]),
                (br, ST.at[pl.ds(misc + 2, fields), mid_rows, :]),
            ])
        ]
        for c in loads:
            c.start()

        barrier = pltpu.get_barrier_semaphore()

        @pl.loop(1, n)
        def _(k):
            other = lax.rem(me + k, n)
            pl.semaphore_signal(
                barrier, inc=1, device_id={"lat": other // n_lon, "lon": lax.rem(other, n_lon)},
                device_id_type=MESH,
            )

        lane = lax.broadcasted_iota(jnp.int32, (wide, cols), 1)
        place = lane & (BLOCK - 1)
        block = lane >> (BLOCK.bit_length() - 1)
        row = lax.broadcasted_iota(jnp.int32, (wide, cols), 0) + lat * rows - PAD
        own = slice(PAD, PAD + rows)
        low = slice(0, PAD)
        high = slice(PAD + rows, wide)
        everything = slice(0, wide)

        def pack(planes):
            height = planes[0].shape[0]
            b = block[:height]
            x = roll_lanes(planes[0], -118)
            for f in range(1, 4):
                x = jnp.where(b == f, roll_lanes(planes[f], BLOCK * f - 118), x)
            return x

        def message(packed, base):
            height = packed[0].shape[0]
            p = place[:height] // 8
            x = roll_lanes(packed[0], -base)
            for j in range(1, len(packed)):
                x = jnp.where(p == j, roll_lanes(packed[j], 8 * j - base), x)
            return x

        def lay(packed):
            return jnp.where(place[: packed.shape[0]] < 10, packed, roll_lanes(packed, 12))

        for ref in (A0, A1):
            ref[:, 0:1] = jnp.zeros((fields, 1, wide, cols), jnp.float32)

        def clear(part):
            A0[:, 1 : levels + 1, part, :] = jnp.zeros((fields, levels, PAD, cols), jnp.float32)
            ST[:, part, :] = jnp.zeros((misc + 2 + fields, PAD, cols), jnp.float32)
            WI[:, part, :] = jnp.zeros((levels, PAD, cols), jnp.int32)
            BI[part, :] = jnp.zeros((PAD, cols), jnp.int32)
            F[:, part, :] = jnp.zeros((2 * fields, PAD, cols), jnp.float32)
            for ref in (RE, RW, FRE, FRW):
                ref[:, part, :] = jnp.zeros((ref.shape[0], PAD, cols), jnp.float32)

        for part in (slice(0, PAD - RIM), slice(PAD + rows + RIM, wide)):
            height = part.stop - part.start
            A0[:, 1 : levels + 1, part, :] = jnp.zeros((fields, levels, height, cols), jnp.float32)
            ST[:, part, :] = jnp.zeros((misc + 2 + fields, height, cols), jnp.float32)
            WI[:, part, :] = jnp.zeros((levels, height, cols), jnp.int32)
            BI[part, :] = jnp.zeros((height, cols), jnp.int32)
            F[:, part, :] = jnp.zeros((2 * fields, height, cols), jnp.float32)
            for ref in (RE, RW, FRE, FRW):
                ref[:, part, :] = jnp.zeros((ref.shape[0], height, cols), jnp.float32)

        @pl.when(lat == 0)
        def _():
            clear(low)

        @pl.when(lat == n_lat - 1)
        def _():
            clear(high)

        angle = math.pi * (row.astype(jnp.float32) + 0.5) / total_rows - math.pi / 2
        SC[2] = coriolis_scale * jnp.sin(angle)

        def remote(src, dst, send, recv, i, to_lat, to_lon):
            return pltpu.make_async_remote_copy(
                src_ref=src, dst_ref=dst, send_sem=send.at[i], recv_sem=recv.at[i],
                device_id={"lat": to_lat, "lon": to_lon}, device_id_type=MESH,
            )

        def filler(count):
            height = max(h for h in range(1, wide + 1) if count % h == 0)
            return ST.at[pl.ds(0, count // height), pl.ds(0, height)]

        class Group:
            def __init__(self, both, up, down, sends, recvs, counts):
                self.copies, self.sends, self.recvs, self.counts = (both, up, down), sends, recvs, counts

            def each(self, action, toward):
                both, up, down = range(3)
                if self.copies[both]:
                    action(both)
                pl.when(lat < n_lat - 1 if toward else lat > 0)(lambda: action(up))
                pl.when(lat > 0 if toward else lat < n_lat - 1)(lambda: action(down))

            def start(self):
                def go(i):
                    for c in self.copies[i]:
                        c.start()

                self.each(go, True)

            def wait(self, sems, toward):
                def done(i):
                    some = filler(self.counts[i])
                    pltpu.make_async_copy(some, some, sems.at[i]).wait()

                self.each(done, toward)

            def finish_recv(self):
                self.wait(self.recvs, False)

            def finish_send(self):
                self.wait(self.sends, True)

        low_rim, high_rim = pl.ds(PAD - RIM, RIM), pl.ds(PAD + rows, RIM)
        top, bottom = pl.ds(rows - RIM, RIM), pl.ds(0, RIM)

        def strip_copies(to_e, to_w, from_e, from_w, send, recv):
            both = [
                remote(to_e, from_w.at[:, mid_rows, :], send, recv, 0, lat, eastward),
                remote(to_w, from_e.at[:, mid_rows, :], send, recv, 0, lat, westward),
            ]
            up = [
                remote(to_e.at[:, top, :], from_w.at[:, low_rim, :], send, recv, 1, lat + 1, eastward),
                remote(to_w.at[:, top, :], from_e.at[:, low_rim, :], send, recv, 1, lat + 1, westward),
            ]
            down = [
                remote(to_e.at[:, bottom, :], from_w.at[:, high_rim, :], send, recv, 2, lat - 1, eastward),
                remote(to_w.at[:, bottom, :], from_e.at[:, high_rim, :], send, recv, 2, lat - 1, westward),
            ]
            return both, up, down

        def rims(src, dst, i, to_lat):
            return [
                remote(fa.at[:, :, src, :], A0.at[:, inner, dst, :], halo_send, halo_recv, i, to_lat, lon),
                remote(du.at[:, src, :], ST.at[pl.ds(0, levels), dst, :], halo_send, halo_recv, i, to_lat, lon),
                remote(dv.at[:, src, :], ST.at[pl.ds(levels, levels), dst, :], halo_send, halo_recv, i, to_lat, lon),
                remote(wm.at[:, src, :], WI.at[:, dst, :], halo_send, halo_recv, i, to_lat, lon),
                remote(bl.at[src, :], BI.at[dst, :], halo_send, halo_recv, i, to_lat, lon),
                remote(vi.at[src, :], ST.at[misc, dst, :], halo_send, halo_recv, i, to_lat, lon),
                remote(br.at[:, src, :], ST.at[pl.ds(misc + 2, fields), dst, :], halo_send, halo_recv, i, to_lat, lon),
            ]

        planes = (fields + 3) * levels + 2 + fields
        halo = Group(
            [], rims(top, low_rim, 1, lat + 1), rims(bottom, high_rim, 2, lat - 1),
            halo_send, halo_recv, (0, planes * RIM, planes * RIM),
        )
        side = Group(
            *strip_copies(ME, MW, RE, RW, side_send, side_recv), side_send, side_recv,
            (2 * messages * rows, 2 * messages * RIM, 2 * messages * RIM),
        )

        pl.semaphore_wait(barrier, n - 1)
        halo.start()

        def convert(part):
            for k in range(levels):
                ST[k, part, :] = 0.5 * ST[k, part, :]
                ST[levels + k, part, :] = 0.5 * ST[levels + k, part, :]
                ST[2 * levels + k, part, :] = WI[k, part, :].astype(jnp.float32)
            ST[misc + 1, part, :] = BI[part, :].astype(jnp.float32)

        def sources(i, part):
            if i < fields * groups:
                f, j = divmod(i, groups)
                return [A0[f, b * groups + j + 1, part, :] for b in range(4)]
            if i < (fields + 3) * groups:
                kind, j = divmod(i - fields * groups, groups)
                return [ST[kind * levels + b * groups + j, part, :] for b in range(4)]
            if i == (fields + 3) * groups:
                v, d = ST[misc, part, :], ST[misc + 1, part, :]
                return [v, d, v, d]
            return [ST[misc + 2 + f, part, :] for f in range(4)]

        loads[1].wait()
        some = filler((3 * levels + 2 + fields) * rows)
        pltpu.make_async_copy(some, some, in_sem.at[2]).wait()
        convert(own)
        for m in range(messages):
            ids = range(4 * m, min(4 * m + 4, strips))
            packed = [pack(sources(i, own)) for i in ids]
            ME[m] = message(packed, 4)
            MW[m] = message(packed, 10)
            for i, x in zip(ids, packed):
                SP[i, own, :] = lay(x)
        side.start()

        def across(x):
            return jnp.concatenate([x] * 4, axis=0).T

        def by_block(t, which):
            height = t.shape[0] // 4
            x = t[:height]
            for r in range(1, 4):
                x = jnp.where(which == r, t[r * height : (r + 1) * height], x)
            return x

        part_of = (lane[:lines] & (q_share - 1)) // per
        part_block = block[:lines]

        def pack_forcing(step, e, i):
            for b in range(n_lat):
                x = at[step, :, b * s_share : (b + 1) * s_share, :].reshape(lines, cols)
                Y[b] = across(x)
                for p in range(per):
                    x = Y[b, pl.ds(p, n_lon, stride=q_share), :]
                    for r in range(1, 4):
                        x = jnp.where(block[:n_lon] == r, Y[b, pl.ds(per * r + p, n_lon, stride=q_share), :], x)
                    SB[e, pl.ds(b * n_lon * 8 + i * per + p, n_lon, stride=8), :] = x

        def unpack_forcing(e, i, to):
            for b in range(n_lat):
                x = jnp.concatenate(
                    [RB[e, pl.ds(b * n_lon * 8 + i * per + p, n_lon, stride=8), :] for p in range(per)], axis=0
                )
                to[pl.ds(b, lines, stride=n_lat), :] = by_block(across(x), part_block)

        def pack_flux(e, i):
            for b in range(n_lat):
                x = by_block(across(FL[pl.ds(b, lines, stride=n_lat), :]), block[:BLOCK])
                for p in range(per):
                    at_row = b * n_lon * 8 + i * per + p
                    SB[e, pl.ds(at_row, n_lon, stride=8), :] = x[p * n_lon : (p + 1) * n_lon]

        def unpack_flux(e, i, step):
            for b in range(n_lat):
                for p in range(per):
                    x = RB[e, pl.ds(b * n_lon * 8 + i * per + p, n_lon, stride=8), :]
                    for r in range(4):
                        Y[b, pl.ds(per * r + p, n_lon, stride=q_share), :] = x
                x = by_block(Y[b].T, part_of)
                flux[step, :, b * s_share : (b + 1) * s_share, :] = x.reshape(fields, s_share, cols)

        def place_of(device, size):
            return pl.ds(pl.multiple_of(device * 8, 8), size)

        def exchange(e, size):
            def send(la, lo):
                pltpu.make_async_remote_copy(
                    src_ref=SB.at[e, place_of(la * n_lon + lo, size)], dst_ref=RB.at[e, place_of(me, size)],
                    send_sem=a2a_send.at[e], recv_sem=a2a_recv.at[e],
                    device_id={"lat": la, "lon": lo}, device_id_type=MESH,
                ).start()

            for dl in range(n_lat):
                la = lax.rem(lat + dl, n_lat)
                least = 1 if dl == 0 else 0
                if n_lon <= 8:
                    for dn in range(least, n_lon):
                        send(la, lax.rem(lon + dn, n_lon))
                else:
                    @pl.loop(least, n_lon)
                    def _(dn):
                        send(la, lax.rem(lon + dn, n_lon))

            RB[e, place_of(me, 8), :] = SB[e, place_of(me, 8), :]

        def all_of(e, size, sem):
            some = pl.ds(0, (n - 1) * size)
            pltpu.make_async_copy(SB.at[e, some], RB.at[e, some], sem.at[e]).wait()

        loads[0].wait()
        pack_forcing(2, 0, 0)
        pack_forcing(1, 0, 1)
        exchange(0, 2 * per)

        def store_flux(A):
            for f in range(fields):
                FL[f * rows : (f + 1) * rows] = A[f, 1, own, :] * ST[2 * levels, own, :]

        pack_forcing(0, 1, 0)
        store_flux(A0)
        pack_flux(1, 1)

        halo.finish_recv()
        for part in (low, high):
            convert(part)
            for i in range(strips):
                SP[i, part, :] = lay(pack(sources(i, part)))

        side.finish_recv()
        between = (place >= 10) & (place < 22)
        half = lane & 15
        for m in range(messages):
            from_e, from_w = RE[m], roll_lanes(RW[m], 6)
            even = jnp.where(half < 6, from_e, from_w)
            odd = jnp.where((half >= 8) & (half < 14), from_e, from_w)
            for p in range(min(4, strips - 4 * m)):
                x = roll_lanes((even, odd)[p % 2], 10 - 8 * p)
                SP[4 * m + p] = jnp.where(between, x, SP[4 * m + p])

        strip_u, strip_v, strip_wet = [(fields + i) * groups for i in range(3)]
        x = SP[(fields + 3) * groups]
        SC[0] = jnp.where((block & 1) == 0, x, roll_lanes(x, BLOCK))
        SC[1] = jnp.where((block & 1) == 1, x, roll_lanes(x, -BLOCK)) - (block * groups).astype(jnp.float32)
        x = SP[(fields + 3) * groups + 1]
        for f in range(fields):
            SG[f] = jnp.where(block == 0, SP[strip_wet] * roll_lanes(x, -BLOCK * f), 0.0)

        half_t = 0.5 * pressure_weight * expansion
        half_s = -0.5 * pressure_weight * contraction
        edge2 = (lane < 2) | (lane >= cols - 2)
        edge4 = (lane < 4) | (lane >= cols - 4)
        keep_low = jnp.where(lat > 0, 1.0, 0.0)
        keep_high = jnp.where(lat < n_lat - 1, 1.0, 0.0)

        def masked(x):
            return jnp.concatenate([x[low] * keep_low, x[own], x[high] * keep_high], axis=0)

        def spatial(w, u, v, extra_u, extra_v, visc, part):
            y = visc * w
            inner_lap = (north(y) + south(y)) - 4.0 * y
            z = lap_weight * w - masked(inner_lap)
            along, across = u * w, v * w
            if extra_u is not None:
                along, across = along + extra_u, across + extra_v
            vertical = north(z + across) + south(z - across)
            z, y, along = z[part], y[part], along[part]
            t = z - inner_lap[part]
            flat = (east(t + along) + west(t - along)) - (roll_lanes(y, -2) + roll_lanes(y, 2))
            return (flat + vertical[part]) - (4.0 * z + 2.0 * y)

        def strip_step(A, B):
            depth, visc, cor = SC[1], SC[0], SC[2]
            w = [[SP[strip_wet + j] * A[f * groups + j] for j in range(groups)] for f in range(fields)]
            sums = []
            for f in (2, 3):
                c = [w[f][groups - 1]]
                for j in range(groups - 2, -1, -1):
                    c.insert(0, c[0] + w[f][j])
                later = 0.0
                for b in range(1, 4):
                    later = later + jnp.where(block < 4 - b, roll_lanes(c[0], -BLOCK * b), 0.0)
                sums.append([x + later for x in c])
            down = []
            for j in range(groups):
                mix = jnp.where(depth > j + 1.0, mixing_rate, 0.0)
                down.append([
                    mix * ((w[f][j + 1] if j < groups - 1 else roll_lanes(w[f][0], -BLOCK)) - w[f][j])
                    for f in range(fields)
                ])
            for j in range(groups):
                drag = jnp.where(depth == j + 1.0, drag_rate, 0.0)
                u, v = SP[strip_u + j], SP[strip_v + j]
                for f in range(fields):
                    h = (half_t, half_s, 0.0, 0.0)[f]
                    eu = h * sums[0][j] if f < 2 else None
                    ev = h * sums[1][j] if f < 2 else None
                    x = w[f][j]
                    new = A[f * groups + j] + spatial(x, u, v, eu, ev, visc, everything)
                    up = down[j - 1][f] if j > 0 else roll_lanes(down[groups - 1][f], BLOCK)
                    new = new + (down[j][f] - up)
                    if f == 2:
                        new = new - (drag * x + cor * w[3][j])
                    if f == 3:
                        new = new - (drag * x - cor * w[2][j])
                    B[f * groups + j] = new
                    J[f * groups + j] = jnp.where(place < 10, new, roll_lanes(new, -12))

        wet_top = 2 * levels

        def begin(A):
            wet = ST[wet_top + levels - 1]
            w = [wet * A[f, levels] for f in range(fields)]
            nothing = jnp.zeros((wide, cols), jnp.float32)
            return (nothing, nothing, *w, nothing, nothing, nothing, nothing)

        def level(A, k, carry, part, write):
            cu, cv, *rest = carry
            w, g = rest[:4], rest[4:]
            kf = jnp.asarray(k, jnp.int32).astype(jnp.float32)
            first = kf + jnp.where(k == 0, 1000.0, 0.0)
            depth, visc, cor = ST[misc + 1], ST[misc], SC[2][part]
            wet_up = ST[wet_top + jnp.where(k == 0, 0, k - 1)]
            mix = jnp.where(depth > first, mixing_rate, 0.0)
            drag = jnp.where(depth[part] == kf + 1.0, drag_rate, 0.0)
            u, v = ST[k], ST[levels + k]
            cu, cv = cu + w[2], cv + w[3]
            w_up = [wet_up * A[f, k] for f in range(fields)]
            g_up = [mix * (w[f] - w_up[f]) for f in range(fields)]
            for f in range(fields):
                h = (half_t, half_s, 0.0, 0.0)[f]
                eu = h * cu if f < 2 else None
                ev = h * cv if f < 2 else None
                new = A[f, k + 1][part] + spatial(w[f], u, v, eu, ev, visc, part)
                new = new + (g[f][part] - g_up[f][part])
                if f == 2:
                    new = new - (drag * w[2][part] + cor * w[3][part])
                if f == 3:
                    new = new - (drag * w[3][part] - cor * w[2][part])
                write(f, k, new)
            return (cu, cv, *w_up, *g_up)

        def sweep(A, carry, first, last, part, write):
            def body(i, carry):
                for j in range(UNROLL):
                    carry = level(A, first - i * UNROLL - j, carry, part, write)
                return carry

            return lax.fori_loop(0, (first - last + 1) // UNROLL, body, carry)

        def fixed(f, k, part, edge, new):
            b = k // groups
            x = pltpu.roll(J[f * groups + lax.rem(k, groups), part, :], 118 - BLOCK * b, 1)
            return jnp.where(edge[part], x, new)

        def surface(A, S, B, R, i):
            for f in range(fields):
                R[f * groups] = R[f * groups] + SG[f] * (FS[i * fields + f] - S[f * groups])
                gain = ST[wet_top] * ST[misc + 2 + f]
                B[f, 1] = B[f, 1] + gain * (F[i * fields + f] - A[f, 1])

        all_of(0, 2 * per, a2a_recv)
        for i in range(2):
            unpack_forcing(0, i, FL)
            for f in range(fields):
                F[i * fields + f, own, :] = FL[f * rows : (f + 1) * rows]
        packed = [pack([F[i * fields + f, own, :] for f in range(4)]) for i in range(2)]
        FE[0] = message(packed, 4)
        FW[0] = message(packed, 10)
        both, up, down = strip_copies(FE, FW, FRE, FRW, f_send, f_recv)
        up = up + [remote(F.at[:, pl.ds(PAD + rows - RIM, RIM), :], F.at[:, low_rim, :], f_send, f_recv, 1, lat + 1, lon)]
        down = down + [remote(F.at[:, pl.ds(PAD, RIM), :], F.at[:, high_rim, :], f_send, f_recv, 2, lat - 1, lon)]
        f_halo = Group(
            both, up, down, f_send, f_recv, (2 * rows, (2 + 2 * fields) * RIM, (2 + 2 * fields) * RIM),
        )
        f_halo.start()
        strip_step(SP, SN)

        def write1(f, k, new):
            A1[f, k + 1] = fixed(f, k, everything, edge2, new)

        sweep(A0, begin(A0), levels - 1, 0, everything, write1)


        exchange(1, 2 * per)

        def write2(f, k, new):
            A0[f, k + 1] = new

        carry = sweep(A1, begin(A1), levels - 1, groups, everything, write2)

        f_halo.finish_recv()
        for i in range(2):
            x = lay(pack([F[i * fields + f] for f in range(4)]))
            x = jnp.where((place >= 10) & (place < 16), roll_lanes(FRE[0], 10 - 8 * i), x)
            x = jnp.where((place >= 16) & (place < 22), roll_lanes(FRW[0], 16 - 8 * i), x)
            for f in range(fields):
                FS[i * fields + f] = roll_lanes(x, -BLOCK * f)
        surface(A0, SP, A1, SN, 0)
        store_flux(A1)
        pack_flux(2, 0)
        exchange(2, per)
        strip_step(SN, SP)
        sweep(A1, carry, groups - 1, 0, everything, write2)
        for f in range(fields):
            A0[f, 1] = fixed(f, 0, everything, edge2, A0[f, 1])
        surface(A1, SN, A0, SP, 1)
        store_flux(A0)
        pack_flux(3, 0)
        exchange(3, per)

        strip_step(SP, SN)

        def write3(f, k, new):
            out[f, k] = fixed(f, k, own, edge4, new)

        sweep(A0, begin(A0), levels - 1, 0, own, write3)
        all_of(1, 2 * per, a2a_recv)
        unpack_forcing(1, 0, FL)
        for f in range(fields):
            gain = ST[wet_top, own, :] * ST[misc + 2 + f, own, :]
            out[f, 0] = out[f, 0] + gain * (FL[f * rows : (f + 1) * rows] - A0[f, 1, own, :])

        unpack_flux(1, 1, 2)
        all_of(2, per, a2a_recv)
        unpack_flux(2, 0, 1)
        all_of(3, per, a2a_recv)
        unpack_flux(3, 0, 0)
        halo.finish_send()
        side.finish_send()
        f_halo.finish_send()
        for e in range(4):
            all_of(e, (2 * per, 2 * per, per, per)[e], a2a_send)

    return kernel


def local(
    final_adjoint, drift_u, drift_v, wet_mask, bottom_level, viscosity, bulk_rate, atmos_adjoint
):
    fields, levels, rows, cols = final_adjoint.shape
    window = atmos_adjoint.shape[0]
    n_lat, n_lon = lax.axis_size("lat"), lax.axis_size("lon")
    n = n_lat * n_lon
    wide = rows + 2 * PAD
    q_share = cols // n_lon
    groups = levels // 4
    strips = (fields + 3) * groups + 2
    messages = -(-strips // 4)

    def buf(*shape):
        return pltpu.VMEM(shape, jnp.float32)

    kernel = make_kernel(n_lat, n_lon, fields, levels, rows, cols, window, q_share)
    f32 = jnp.float32
    anywhere = pl.BlockSpec(memory_space=pl.ANY)
    return pl.pallas_call(
        kernel,
        out_shape=(
            pltpu.VMEM(final_adjoint.shape, f32),
            pltpu.VMEM(atmos_adjoint.shape, f32),
        ),
        in_specs=[anywhere] * 8,
        out_specs=(pl.BlockSpec(memory_space=pltpu.VMEM),) * 2,
        scratch_shapes=[
            buf(window, fields, rows, cols),
            buf(fields, levels + 1, wide, cols), buf(fields, levels + 1, wide, cols),
            buf(3 * levels + 2 + fields, wide, cols),
            pltpu.VMEM((levels, wide, cols), jnp.int32), pltpu.VMEM((wide, cols), jnp.int32),
            buf(strips, wide, cols), buf(fields * groups, wide, cols),
            buf(3, wide, cols), buf(fields, wide, cols), buf(fields * groups, wide, cols),
            buf(messages, rows, cols), buf(messages, rows, cols),
            buf(messages, wide, cols), buf(messages, wide, cols),
            buf(2 * fields, wide, cols), buf(2 * fields, wide, cols),
            buf(1, rows, cols), buf(1, rows, cols), buf(1, wide, cols), buf(1, wide, cols),
            buf(n_lat, cols, cols), buf(fields * rows, cols), buf(4, n * 8, cols), buf(4, n * 8, cols),
            *[pltpu.SemaphoreType.DMA((3,))] * 6,
            pltpu.SemaphoreType.DMA((4,)), pltpu.SemaphoreType.DMA((4,)), pltpu.SemaphoreType.DMA((3,)),
        ],
        compiler_params=pltpu.CompilerParams(
            collective_id=0, has_side_effects=True, vmem_limit_bytes=60 * 1024 * 1024
        ),
    )(final_adjoint, drift_u, drift_v, wet_mask, bottom_level, viscosity, bulk_rate, atmos_adjoint)


def solution(mesh):
    in_specs = (
        P(None, None, "lat", "lon"),
        P(None, "lat", "lon"),
        P(None, "lat", "lon"),
        P(None, "lat", "lon"),
        P("lat", "lon"),
        P("lat", "lon"),
        P(None, "lat", "lon"),
        P(None, None, "lat", "lon"),
    )
    out_specs = (P(None, None, "lat", "lon"), P(None, None, "lat", "lon"))
    return jax.shard_map(local, mesh=mesh, in_specs=in_specs, out_specs=out_specs, check_vma=False)
```

```python
import math

import jax
import jax.numpy as jnp
from jax import lax
from jax.experimental import pallas as pl
from jax.experimental.pallas import tpu as pltpu
from jax.sharding import PartitionSpec as P

lap_weight = 0.04
mixing_rate = 0.15
drag_rate = 0.2
expansion = 0.2
contraction = 0.15
pressure_weight = 0.1
coriolis_scale = 0.2

MESH = pl.DeviceIdType.MESH
PAD = 8
RIM = 6
BLOCK = 32
UNROLL = 3


def roll_lanes(x, shift):
    shift = shift % x.shape[-1]
    return pltpu.roll(x, shift, x.ndim - 1) if shift else x


def east(x):
    return roll_lanes(x, -1)


def west(x):
    return roll_lanes(x, 1)


def north(x):
    return pltpu.roll(x, x.shape[0] - 1, 0)


def south(x):
    return pltpu.roll(x, 1, 0)


def make_kernel(n_lat, n_lon, fields, levels, rows, cols, window, q_share):
    n = n_lat * n_lon
    wide = rows + 2 * PAD
    total_rows = rows * n_lat
    s_share = rows // n_lat
    lines = fields * s_share
    per = BLOCK // n_lon
    misc = 3 * levels
    groups = levels // 4
    strips = (fields + 3) * groups + 2
    messages = -(-strips // 4)

    def kernel(
        fa, du, dv, wm, bl, vi, br, at_hbm,
        out, flux,
        at, A0, A1, ST, WI, BI, SP, SN, SC, SG, J, ME, MW, RE, RW, F, FS, FE, FW, FRE, FRW,
        Y, FL, SB, RB,
        halo_send, halo_recv, side_send, side_recv, f_send, f_recv, a2a_send, a2a_recv, in_sem,
    ):
        lat = lax.axis_index("lat")
        lon = lax.axis_index("lon")
        me = lat * n_lon + lon
        eastward = lax.rem(lon + 1, n_lon)
        westward = lax.rem(lon + n_lon - 1, n_lon)

        mid_rows = pl.ds(PAD, rows)
        inner = pl.ds(1, levels)
        loads = [
            pltpu.make_async_copy(src, dst, in_sem.at[min(i, 2)])
            for i, (src, dst) in enumerate([
                (at_hbm, at),
                (fa, A0.at[:, inner, mid_rows, :]),
                (du, ST.at[pl.ds(0, levels), mid_rows, :]),
                (dv, ST.at[pl.ds(levels, levels), mid_rows, :]),
                (wm, WI.at[:, mid_rows, :]),
                (bl, BI.at[mid_rows, :]),
                (vi, ST.at[misc, mid_rows, :]),
                (br, ST.at[pl.ds(misc + 2, fields), mid_rows, :]),
            ])
        ]
        for c in loads:
            c.start()

        barrier = pltpu.get_barrier_semaphore()

        @pl.loop(1, n)
        def _(k):
            other = lax.rem(me + k, n)
            pl.semaphore_signal(
                barrier, inc=1, device_id={"lat": other // n_lon, "lon": lax.rem(other, n_lon)},
                device_id_type=MESH,
            )

        lane = lax.broadcasted_iota(jnp.int32, (wide, cols), 1)
        place = lane & (BLOCK - 1)
        block = lane >> (BLOCK.bit_length() - 1)
        row = lax.broadcasted_iota(jnp.int32, (wide, cols), 0) + lat * rows - PAD
        own = slice(PAD, PAD + rows)
        low = slice(0, PAD)
        high = slice(PAD + rows, wide)
        everything = slice(0, wide)

        def pack(planes):
            height = planes[0].shape[0]
            b = block[:height]
            x = roll_lanes(planes[0], -118)
            for f in range(1, 4):
                x = jnp.where(b == f, roll_lanes(planes[f], BLOCK * f - 118), x)
            return x

        def message(packed, base):
            height = packed[0].shape[0]
            p = place[:height] // 8
            x = roll_lanes(packed[0], -base)
            for j in range(1, len(packed)):
                x = jnp.where(p == j, roll_lanes(packed[j], 8 * j - base), x)
            return x

        def lay(packed):
            return jnp.where(place[: packed.shape[0]] < 10, packed, roll_lanes(packed, 12))

        for ref in (A0, A1):
            ref[:, 0:1] = jnp.zeros((fields, 1, wide, cols), jnp.float32)

        def clear(part):
            A0[:, 1 : levels + 1, part, :] = jnp.zeros((fields, levels, PAD, cols), jnp.float32)
            ST[:, part, :] = jnp.zeros((misc + 2 + fields, PAD, cols), jnp.float32)
            WI[:, part, :] = jnp.zeros((levels, PAD, cols), jnp.int32)
            BI[part, :] = jnp.zeros((PAD, cols), jnp.int32)
            F[:, part, :] = jnp.zeros((2 * fields, PAD, cols), jnp.float32)
            for ref in (RE, RW, FRE, FRW):
                ref[:, part, :] = jnp.zeros((ref.shape[0], PAD, cols), jnp.float32)

        for part in (slice(0, PAD - RIM), slice(PAD + rows + RIM, wide)):
            height = part.stop - part.start
            A0[:, 1 : levels + 1, part, :] = jnp.zeros((fields, levels, height, cols), jnp.float32)
            ST[:, part, :] = jnp.zeros((misc + 2 + fields, height, cols), jnp.float32)
            WI[:, part, :] = jnp.zeros((levels, height, cols), jnp.int32)
            BI[part, :] = jnp.zeros((height, cols), jnp.int32)
            F[:, part, :] = jnp.zeros((2 * fields, height, cols), jnp.float32)
            for ref in (RE, RW, FRE, FRW):
                ref[:, part, :] = jnp.zeros((ref.shape[0], height, cols), jnp.float32)

        @pl.when(lat == 0)
        def _():
            clear(low)

        @pl.when(lat == n_lat - 1)
        def _():
            clear(high)

        angle = math.pi * (row.astype(jnp.float32) + 0.5) / total_rows - math.pi / 2
        SC[2] = coriolis_scale * jnp.sin(angle)

        def remote(src, dst, send, recv, i, to_lat, to_lon):
            return pltpu.make_async_remote_copy(
                src_ref=src, dst_ref=dst, send_sem=send.at[i], recv_sem=recv.at[i],
                device_id={"lat": to_lat, "lon": to_lon}, device_id_type=MESH,
            )

        def filler(count):
            height = max(h for h in range(1, wide + 1) if count % h == 0)
            return ST.at[pl.ds(0, count // height), pl.ds(0, height)]

        class Group:
            def __init__(self, both, up, down, sends, recvs, counts):
                self.copies, self.sends, self.recvs, self.counts = (both, up, down), sends, recvs, counts

            def each(self, action, toward):
                both, up, down = range(3)
                if self.copies[both]:
                    action(both)
                pl.when(lat < n_lat - 1 if toward else lat > 0)(lambda: action(up))
                pl.when(lat > 0 if toward else lat < n_lat - 1)(lambda: action(down))

            def start(self):
                def go(i):
                    for c in self.copies[i]:
                        c.start()

                self.each(go, True)

            def wait(self, sems, toward):
                def done(i):
                    some = filler(self.counts[i])
                    pltpu.make_async_copy(some, some, sems.at[i]).wait()

                self.each(done, toward)

            def finish_recv(self):
                self.wait(self.recvs, False)

            def finish_send(self):
                self.wait(self.sends, True)

        low_rim, high_rim = pl.ds(PAD - RIM, RIM), pl.ds(PAD + rows, RIM)
        top, bottom = pl.ds(rows - RIM, RIM), pl.ds(0, RIM)

        def strip_copies(to_e, to_w, from_e, from_w, send, recv):
            both = [
                remote(to_e, from_w.at[:, mid_rows, :], send, recv, 0, lat, eastward),
                remote(to_w, from_e.at[:, mid_rows, :], send, recv, 0, lat, westward),
            ]
            up = [
                remote(to_e.at[:, top, :], from_w.at[:, low_rim, :], send, recv, 1, lat + 1, eastward),
                remote(to_w.at[:, top, :], from_e.at[:, low_rim, :], send, recv, 1, lat + 1, westward),
            ]
            down = [
                remote(to_e.at[:, bottom, :], from_w.at[:, high_rim, :], send, recv, 2, lat - 1, eastward),
                remote(to_w.at[:, bottom, :], from_e.at[:, high_rim, :], send, recv, 2, lat - 1, westward),
            ]
            return both, up, down

        def rims(src, dst, i, to_lat):
            return [
                remote(fa.at[:, :, src, :], A0.at[:, inner, dst, :], halo_send, halo_recv, i, to_lat, lon),
                remote(du.at[:, src, :], ST.at[pl.ds(0, levels), dst, :], halo_send, halo_recv, i, to_lat, lon),
                remote(dv.at[:, src, :], ST.at[pl.ds(levels, levels), dst, :], halo_send, halo_recv, i, to_lat, lon),
                remote(wm.at[:, src, :], WI.at[:, dst, :], halo_send, halo_recv, i, to_lat, lon),
                remote(bl.at[src, :], BI.at[dst, :], halo_send, halo_recv, i, to_lat, lon),
                remote(vi.at[src, :], ST.at[misc, dst, :], halo_send, halo_recv, i, to_lat, lon),
                remote(br.at[:, src, :], ST.at[pl.ds(misc + 2, fields), dst, :], halo_send, halo_recv, i, to_lat, lon),
            ]

        planes = (fields + 3) * levels + 2 + fields
        halo = Group(
            [], rims(top, low_rim, 1, lat + 1), rims(bottom, high_rim, 2, lat - 1),
            halo_send, halo_recv, (0, planes * RIM, planes * RIM),
        )
        side = Group(
            *strip_copies(ME, MW, RE, RW, side_send, side_recv), side_send, side_recv,
            (2 * messages * rows, 2 * messages * RIM, 2 * messages * RIM),
        )

        def across(x):
            return jnp.concatenate([x] * 4, axis=0).T

        def by_block(t, which):
            height = t.shape[0] // 4
            x = t[:height]
            for r in range(1, 4):
                x = jnp.where(which == r, t[r * height : (r + 1) * height], x)
            return x

        part_of = (lane[:lines] & (q_share - 1)) // per
        part_block = block[:lines]

        def pack_forcing(step, e, i):
            for b in range(n_lat):
                x = at[step, :, b * s_share : (b + 1) * s_share, :].reshape(lines, cols)
                Y[b] = across(x)
                for p in range(per):
                    x = Y[b, pl.ds(p, n_lon, stride=q_share), :]
                    for r in range(1, 4):
                        x = jnp.where(block[:n_lon] == r, Y[b, pl.ds(per * r + p, n_lon, stride=q_share), :], x)
                    SB[e, pl.ds(b * n_lon * 8 + i * per + p, n_lon, stride=8), :] = x

        def unpack_forcing(e, i, to):
            for b in range(n_lat):
                x = jnp.concatenate(
                    [RB[e, pl.ds(b * n_lon * 8 + i * per + p, n_lon, stride=8), :] for p in range(per)], axis=0
                )
                to[pl.ds(b, lines, stride=n_lat), :] = by_block(across(x), part_block)

        def pack_flux(e, i):
            for b in range(n_lat):
                x = by_block(across(FL[pl.ds(b, lines, stride=n_lat), :]), block[:BLOCK])
                for p in range(per):
                    at_row = b * n_lon * 8 + i * per + p
                    SB[e, pl.ds(at_row, n_lon, stride=8), :] = x[p * n_lon : (p + 1) * n_lon]

        def unpack_flux(e, i, step):
            for b in range(n_lat):
                for p in range(per):
                    x = RB[e, pl.ds(b * n_lon * 8 + i * per + p, n_lon, stride=8), :]
                    for r in range(4):
                        Y[b, pl.ds(per * r + p, n_lon, stride=q_share), :] = x
                x = by_block(Y[b].T, part_of)
                flux[step, :, b * s_share : (b + 1) * s_share, :] = x.reshape(fields, s_share, cols)

        def place_of(device, size):
            return pl.ds(pl.multiple_of(device * 8, 8), size)

        def exchange(e, size):
            def send(la, lo):
                pltpu.make_async_remote_copy(
                    src_ref=SB.at[e, place_of(la * n_lon + lo, size)], dst_ref=RB.at[e, place_of(me, size)],
                    send_sem=a2a_send.at[e], recv_sem=a2a_recv.at[e],
                    device_id={"lat": la, "lon": lo}, device_id_type=MESH,
                ).start()

            for dl in range(n_lat):
                la = lax.rem(lat + dl, n_lat)
                least = 1 if dl == 0 else 0
                if n_lon <= 8:
                    for dn in range(least, n_lon):
                        send(la, lax.rem(lon + dn, n_lon))
                else:
                    @pl.loop(least, n_lon)
                    def _(dn):
                        send(la, lax.rem(lon + dn, n_lon))

            RB[e, place_of(me, 8), :] = SB[e, place_of(me, 8), :]

        def all_of(e, size, sem):
            some = pl.ds(0, (n - 1) * size)
            pltpu.make_async_copy(SB.at[e, some], RB.at[e, some], sem.at[e]).wait()

        loads[0].wait()
        pack_forcing(2, 0, 0)
        pack_forcing(1, 0, 1)

        def convert(part):
            for k in range(levels):
                ST[k, part, :] = 0.5 * ST[k, part, :]
                ST[levels + k, part, :] = 0.5 * ST[levels + k, part, :]
                ST[2 * levels + k, part, :] = WI[k, part, :].astype(jnp.float32)
            ST[misc + 1, part, :] = BI[part, :].astype(jnp.float32)

        def sources(i, part):
            if i < fields * groups:
                f, j = divmod(i, groups)
                return [A0[f, b * groups + j + 1, part, :] for b in range(4)]
            if i < (fields + 3) * groups:
                kind, j = divmod(i - fields * groups, groups)
                return [ST[kind * levels + b * groups + j, part, :] for b in range(4)]
            if i == (fields + 3) * groups:
                v, d = ST[misc, part, :], ST[misc + 1, part, :]
                return [v, d, v, d]
            return [ST[misc + 2 + f, part, :] for f in range(4)]

        loads[1].wait()
        some = filler((3 * levels + 2 + fields) * rows)
        pltpu.make_async_copy(some, some, in_sem.at[2]).wait()
        convert(own)
        for m in range(messages):
            ids = range(4 * m, min(4 * m + 4, strips))
            packed = [pack(sources(i, own)) for i in ids]
            ME[m] = message(packed, 4)
            MW[m] = message(packed, 10)
            for i, x in zip(ids, packed):
                SP[i, own, :] = lay(x)
        pl.semaphore_wait(barrier, n - 1)
        exchange(0, 2 * per)

        side.start()
        halo.start()

        def store_flux(A):
            for f in range(fields):
                FL[f * rows : (f + 1) * rows] = A[f, 1, own, :] * ST[2 * levels, own, :]

        pack_forcing(0, 1, 0)
        store_flux(A0)
        pack_flux(1, 1)

        halo.finish_recv()
        for part in (low, high):
            convert(part)
            for i in range(strips):
                SP[i, part, :] = lay(pack(sources(i, part)))

        side.finish_recv()
        between = (place >= 10) & (place < 22)
        half = lane & 15
        for m in range(messages):
            from_e, from_w = RE[m], roll_lanes(RW[m], 6)
            even = jnp.where(half < 6, from_e, from_w)
            odd = jnp.where((half >= 8) & (half < 14), from_e, from_w)
            for p in range(min(4, strips - 4 * m)):
                x = roll_lanes((even, odd)[p % 2], 10 - 8 * p)
                SP[4 * m + p] = jnp.where(between, x, SP[4 * m + p])

        strip_u, strip_v, strip_wet = [(fields + i) * groups for i in range(3)]
        x = SP[(fields + 3) * groups]
        SC[0] = jnp.where((block & 1) == 0, x, roll_lanes(x, BLOCK))
        SC[1] = jnp.where((block & 1) == 1, x, roll_lanes(x, -BLOCK)) - (block * groups).astype(jnp.float32)
        x = SP[(fields + 3) * groups + 1]
        for f in range(fields):
            SG[f] = jnp.where(block == 0, SP[strip_wet] * roll_lanes(x, -BLOCK * f), 0.0)

        half_t = 0.5 * pressure_weight * expansion
        half_s = -0.5 * pressure_weight * contraction
        edge2 = (lane < 2) | (lane >= cols - 2)
        edge4 = (lane < 4) | (lane >= cols - 4)
        keep_low = jnp.where(lat > 0, 1.0, 0.0)
        keep_high = jnp.where(lat < n_lat - 1, 1.0, 0.0)

        def masked(x):
            return jnp.concatenate([x[low] * keep_low, x[own], x[high] * keep_high], axis=0)

        def spatial(w, u, v, extra_u, extra_v, visc, part):
            y = visc * w
            inner_lap = (north(y) + south(y)) - 4.0 * y
            z = lap_weight * w - masked(inner_lap)
            along, across = u * w, v * w
            if extra_u is not None:
                along, across = along + extra_u, across + extra_v
            vertical = north(z + across) + south(z - across)
            z, y, along = z[part], y[part], along[part]
            t = z - inner_lap[part]
            flat = (east(t + along) + west(t - along)) - (roll_lanes(y, -2) + roll_lanes(y, 2))
            return (flat + vertical[part]) - (4.0 * z + 2.0 * y)

        def strip_step(A, B):
            depth, visc, cor = SC[1], SC[0], SC[2]
            w = [[SP[strip_wet + j] * A[f * groups + j] for j in range(groups)] for f in range(fields)]
            sums = []
            for f in (2, 3):
                c = [w[f][groups - 1]]
                for j in range(groups - 2, -1, -1):
                    c.insert(0, c[0] + w[f][j])
                later = 0.0
                for b in range(1, 4):
                    later = later + jnp.where(block < 4 - b, roll_lanes(c[0], -BLOCK * b), 0.0)
                sums.append([x + later for x in c])
            down = []
            for j in range(groups):
                mix = jnp.where(depth > j + 1.0, mixing_rate, 0.0)
                down.append([
                    mix * ((w[f][j + 1] if j < groups - 1 else roll_lanes(w[f][0], -BLOCK)) - w[f][j])
                    for f in range(fields)
                ])
            for j in range(groups):
                drag = jnp.where(depth == j + 1.0, drag_rate, 0.0)
                u, v = SP[strip_u + j], SP[strip_v + j]
                for f in range(fields):
                    h = (half_t, half_s, 0.0, 0.0)[f]
                    eu = h * sums[0][j] if f < 2 else None
                    ev = h * sums[1][j] if f < 2 else None
                    x = w[f][j]
                    new = A[f * groups + j] + spatial(x, u, v, eu, ev, visc, everything)
                    up = down[j - 1][f] if j > 0 else roll_lanes(down[groups - 1][f], BLOCK)
                    new = new + (down[j][f] - up)
                    if f == 2:
                        new = new - (drag * x + cor * w[3][j])
                    if f == 3:
                        new = new - (drag * x - cor * w[2][j])
                    B[f * groups + j] = new
                    J[f * groups + j] = jnp.where(place < 10, new, roll_lanes(new, -12))

        wet_top = 2 * levels

        def begin(A):
            wet = ST[wet_top + levels - 1]
            w = [wet * A[f, levels] for f in range(fields)]
            nothing = jnp.zeros((wide, cols), jnp.float32)
            return (nothing, nothing, *w, nothing, nothing, nothing, nothing)

        def level(A, k, carry, part, write):
            cu, cv, *rest = carry
            w, g = rest[:4], rest[4:]
            kf = jnp.asarray(k, jnp.int32).astype(jnp.float32)
            first = kf + jnp.where(k == 0, 1000.0, 0.0)
            depth, visc, cor = ST[misc + 1], ST[misc], SC[2][part]
            wet_up = ST[wet_top + jnp.where(k == 0, 0, k - 1)]
            mix = jnp.where(depth > first, mixing_rate, 0.0)
            drag = jnp.where(depth[part] == kf + 1.0, drag_rate, 0.0)
            u, v = ST[k], ST[levels + k]
            cu, cv = cu + w[2], cv + w[3]
            w_up = [wet_up * A[f, k] for f in range(fields)]
            g_up = [mix * (w[f] - w_up[f]) for f in range(fields)]
            for f in range(fields):
                h = (half_t, half_s, 0.0, 0.0)[f]
                eu = h * cu if f < 2 else None
                ev = h * cv if f < 2 else None
                new = A[f, k + 1][part] + spatial(w[f], u, v, eu, ev, visc, part)
                new = new + (g[f][part] - g_up[f][part])
                if f == 2:
                    new = new - (drag * w[2][part] + cor * w[3][part])
                if f == 3:
                    new = new - (drag * w[3][part] - cor * w[2][part])
                write(f, k, new)
            return (cu, cv, *w_up, *g_up)

        def sweep(A, carry, first, last, part, write):
            def body(i, carry):
                for j in range(UNROLL):
                    carry = level(A, first - i * UNROLL - j, carry, part, write)
                return carry

            return lax.fori_loop(0, (first - last + 1) // UNROLL, body, carry)

        def fixed(f, k, part, edge, new):
            b = k // groups
            x = pltpu.roll(J[f * groups + lax.rem(k, groups), part, :], 118 - BLOCK * b, 1)
            return jnp.where(edge[part], x, new)

        def surface(A, S, B, R, i):
            for f in range(fields):
                R[f * groups] = R[f * groups] + SG[f] * (FS[i * fields + f] - S[f * groups])
                gain = ST[wet_top] * ST[misc + 2 + f]
                B[f, 1] = B[f, 1] + gain * (F[i * fields + f] - A[f, 1])

        all_of(0, 2 * per, a2a_recv)
        for i in range(2):
            unpack_forcing(0, i, FL)
            for f in range(fields):
                F[i * fields + f, own, :] = FL[f * rows : (f + 1) * rows]
        packed = [pack([F[i * fields + f, own, :] for f in range(4)]) for i in range(2)]
        FE[0] = message(packed, 4)
        FW[0] = message(packed, 10)
        both, up, down = strip_copies(FE, FW, FRE, FRW, f_send, f_recv)
        up = up + [remote(F.at[:, pl.ds(PAD + rows - RIM, RIM), :], F.at[:, low_rim, :], f_send, f_recv, 1, lat + 1, lon)]
        down = down + [remote(F.at[:, pl.ds(PAD, RIM), :], F.at[:, high_rim, :], f_send, f_recv, 2, lat - 1, lon)]
        f_halo = Group(
            both, up, down, f_send, f_recv, (2 * rows, (2 + 2 * fields) * RIM, (2 + 2 * fields) * RIM),
        )
        f_halo.start()
        exchange(1, 2 * per)
        strip_step(SP, SN)

        def write1(f, k, new):
            A1[f, k + 1] = fixed(f, k, everything, edge2, new)

        sweep(A0, begin(A0), levels - 1, 0, everything, write1)


        def write2(f, k, new):
            A0[f, k + 1] = new

        carry = sweep(A1, begin(A1), levels - 1, groups, everything, write2)

        f_halo.finish_recv()
        for i in range(2):
            x = lay(pack([F[i * fields + f] for f in range(4)]))
            x = jnp.where((place >= 10) & (place < 16), roll_lanes(FRE[0], 10 - 8 * i), x)
            x = jnp.where((place >= 16) & (place < 22), roll_lanes(FRW[0], 16 - 8 * i), x)
            for f in range(fields):
                FS[i * fields + f] = roll_lanes(x, -BLOCK * f)
        surface(A0, SP, A1, SN, 0)
        store_flux(A1)
        pack_flux(2, 0)
        exchange(2, per)
        strip_step(SN, SP)
        sweep(A1, carry, groups - 1, 0, everything, write2)
        for f in range(fields):
            A0[f, 1] = fixed(f, 0, everything, edge2, A0[f, 1])
        surface(A1, SN, A0, SP, 1)
        store_flux(A0)
        pack_flux(3, 0)
        exchange(3, per)

        strip_step(SP, SN)

        def write3(f, k, new):
            out[f, k] = fixed(f, k, own, edge4, new)

        sweep(A0, begin(A0), levels - 1, 0, own, write3)
        all_of(1, 2 * per, a2a_recv)
        unpack_forcing(1, 0, FL)
        for f in range(fields):
            gain = ST[wet_top, own, :] * ST[misc + 2 + f, own, :]
            out[f, 0] = out[f, 0] + gain * (FL[f * rows : (f + 1) * rows] - A0[f, 1, own, :])

        unpack_flux(1, 1, 2)
        all_of(2, per, a2a_recv)
        unpack_flux(2, 0, 1)
        all_of(3, per, a2a_recv)
        unpack_flux(3, 0, 0)
        halo.finish_send()
        side.finish_send()
        f_halo.finish_send()
        for e in range(4):
            all_of(e, (2 * per, 2 * per, per, per)[e], a2a_send)

    return kernel


def local(
    final_adjoint, drift_u, drift_v, wet_mask, bottom_level, viscosity, bulk_rate, atmos_adjoint
):
    fields, levels, rows, cols = final_adjoint.shape
    window = atmos_adjoint.shape[0]
    n_lat, n_lon = lax.axis_size("lat"), lax.axis_size("lon")
    n = n_lat * n_lon
    wide = rows + 2 * PAD
    q_share = cols // n_lon
    groups = levels // 4
    strips = (fields + 3) * groups + 2
    messages = -(-strips // 4)

    def buf(*shape):
        return pltpu.VMEM(shape, jnp.float32)

    kernel = make_kernel(n_lat, n_lon, fields, levels, rows, cols, window, q_share)
    f32 = jnp.float32
    anywhere = pl.BlockSpec(memory_space=pl.ANY)
    return pl.pallas_call(
        kernel,
        out_shape=(
            pltpu.VMEM(final_adjoint.shape, f32),
            pltpu.VMEM(atmos_adjoint.shape, f32),
        ),
        in_specs=[anywhere] * 8,
        out_specs=(pl.BlockSpec(memory_space=pltpu.VMEM),) * 2,
        scratch_shapes=[
            buf(window, fields, rows, cols),
            buf(fields, levels + 1, wide, cols), buf(fields, levels + 1, wide, cols),
            buf(3 * levels + 2 + fields, wide, cols),
            pltpu.VMEM((levels, wide, cols), jnp.int32), pltpu.VMEM((wide, cols), jnp.int32),
            buf(strips, wide, cols), buf(fields * groups, wide, cols),
            buf(3, wide, cols), buf(fields, wide, cols), buf(fields * groups, wide, cols),
            buf(messages, rows, cols), buf(messages, rows, cols),
            buf(messages, wide, cols), buf(messages, wide, cols),
            buf(2 * fields, wide, cols), buf(2 * fields, wide, cols),
            buf(1, rows, cols), buf(1, rows, cols), buf(1, wide, cols), buf(1, wide, cols),
            buf(n_lat, cols, cols), buf(fields * rows, cols), buf(4, n * 8, cols), buf(4, n * 8, cols),
            *[pltpu.SemaphoreType.DMA((3,))] * 6,
            pltpu.SemaphoreType.DMA((4,)), pltpu.SemaphoreType.DMA((4,)), pltpu.SemaphoreType.DMA((3,)),
        ],
        compiler_params=pltpu.CompilerParams(
            collective_id=0, has_side_effects=True, vmem_limit_bytes=60 * 1024 * 1024
        ),
    )(final_adjoint, drift_u, drift_v, wet_mask, bottom_level, viscosity, bulk_rate, atmos_adjoint)


def solution(mesh):
    in_specs = (
        P(None, None, "lat", "lon"),
        P(None, "lat", "lon"),
        P(None, "lat", "lon"),
        P(None, "lat", "lon"),
        P("lat", "lon"),
        P("lat", "lon"),
        P(None, "lat", "lon"),
        P(None, None, "lat", "lon"),
    )
    out_specs = (P(None, None, "lat", "lon"), P(None, None, "lat", "lon"))
    return jax.shard_map(local, mesh=mesh, in_specs=in_specs, out_specs=out_specs, check_vma=False)
```

```python
import math

import jax
import jax.numpy as jnp
from jax import lax
from jax.experimental import pallas as pl
from jax.experimental.pallas import tpu as pltpu
from jax.sharding import PartitionSpec as P

lap_weight = 0.04
mixing_rate = 0.15
drag_rate = 0.2
expansion = 0.2
contraction = 0.15
pressure_weight = 0.1
coriolis_scale = 0.2

MESH = pl.DeviceIdType.MESH
PAD = 8
RIM = 6
BLOCK = 32
UNROLL = 3


def roll_lanes(x, shift):
    shift = shift % x.shape[-1]
    return pltpu.roll(x, shift, x.ndim - 1) if shift else x


def east(x):
    return roll_lanes(x, -1)


def west(x):
    return roll_lanes(x, 1)


def north(x):
    return pltpu.roll(x, x.shape[0] - 1, 0)


def south(x):
    return pltpu.roll(x, 1, 0)


def make_kernel(n_lat, n_lon, fields, levels, rows, cols, window, q_share):
    n = n_lat * n_lon
    wide = rows + 2 * PAD
    total_rows = rows * n_lat
    s_share = rows // n_lat
    lines = fields * s_share
    per = BLOCK // n_lon
    misc = 3 * levels
    groups = levels // 4
    strips = (fields + 3) * groups + 2
    messages = -(-strips // 4)

    def kernel(
        fa, du, dv, wm, bl, vi, br, at_hbm,
        out, flux,
        at, A0, A1, ST, WI, BI, SP, SN, SC, SG, J, ME, MW, RE, RW, F, FS, FE, FW, FRE, FRW,
        Y, FL, SB, RB,
        halo_send, halo_recv, side_send, side_recv, f_send, f_recv, a2a_send, a2a_recv, in_sem,
    ):
        lat = lax.axis_index("lat")
        lon = lax.axis_index("lon")
        me = lat * n_lon + lon
        eastward = lax.rem(lon + 1, n_lon)
        westward = lax.rem(lon + n_lon - 1, n_lon)

        mid_rows = pl.ds(PAD, rows)
        inner = pl.ds(1, levels)
        loads = [
            pltpu.make_async_copy(src, dst, in_sem.at[min(i, 2)])
            for i, (src, dst) in enumerate([
                (at_hbm, at),
                (fa, A0.at[:, inner, mid_rows, :]),
                (du, ST.at[pl.ds(0, levels), mid_rows, :]),
                (dv, ST.at[pl.ds(levels, levels), mid_rows, :]),
                (wm, WI.at[:, mid_rows, :]),
                (bl, BI.at[mid_rows, :]),
                (vi, ST.at[misc, mid_rows, :]),
                (br, ST.at[pl.ds(misc + 2, fields), mid_rows, :]),
            ])
        ]
        for c in loads:
            c.start()

        barrier = pltpu.get_barrier_semaphore()

        @pl.loop(1, n)
        def _(k):
            other = lax.rem(me + k, n)
            pl.semaphore_signal(
                barrier, inc=1, device_id={"lat": other // n_lon, "lon": lax.rem(other, n_lon)},
                device_id_type=MESH,
            )

        lane = lax.broadcasted_iota(jnp.int32, (wide, cols), 1)
        place = lane & (BLOCK - 1)
        block = lane >> (BLOCK.bit_length() - 1)
        row = lax.broadcasted_iota(jnp.int32, (wide, cols), 0) + lat * rows - PAD
        own = slice(PAD, PAD + rows)
        low = slice(0, PAD)
        high = slice(PAD + rows, wide)
        everything = slice(0, wide)

        def pack(planes):
            height = planes[0].shape[0]
            b = block[:height]
            x = roll_lanes(planes[0], -118)
            for f in range(1, 4):
                x = jnp.where(b == f, roll_lanes(planes[f], BLOCK * f - 118), x)
            return x

        def message(packed, base):
            height = packed[0].shape[0]
            p = place[:height] // 8
            x = roll_lanes(packed[0], -base)
            for j in range(1, len(packed)):
                x = jnp.where(p == j, roll_lanes(packed[j], 8 * j - base), x)
            return x

        def lay(packed):
            return jnp.where(place[: packed.shape[0]] < 10, packed, roll_lanes(packed, 12))

        for ref in (A0, A1):
            ref[:, 0:1] = jnp.zeros((fields, 1, wide, cols), jnp.float32)

        def clear(part):
            A0[:, 1 : levels + 1, part, :] = jnp.zeros((fields, levels, PAD, cols), jnp.float32)
            ST[:, part, :] = jnp.zeros((misc + 2 + fields, PAD, cols), jnp.float32)
            WI[:, part, :] = jnp.zeros((levels, PAD, cols), jnp.int32)
            BI[part, :] = jnp.zeros((PAD, cols), jnp.int32)
            F[:, part, :] = jnp.zeros((2 * fields, PAD, cols), jnp.float32)
            for ref in (RE, RW, FRE, FRW):
                ref[:, part, :] = jnp.zeros((ref.shape[0], PAD, cols), jnp.float32)

        for part in (slice(0, PAD - RIM), slice(PAD + rows + RIM, wide)):
            height = part.stop - part.start
            A0[:, 1 : levels + 1, part, :] = jnp.zeros((fields, levels, height, cols), jnp.float32)
            ST[:, part, :] = jnp.zeros((misc + 2 + fields, height, cols), jnp.float32)
            WI[:, part, :] = jnp.zeros((levels, height, cols), jnp.int32)
            BI[part, :] = jnp.zeros((height, cols), jnp.int32)
            F[:, part, :] = jnp.zeros((2 * fields, height, cols), jnp.float32)
            for ref in (RE, RW, FRE, FRW):
                ref[:, part, :] = jnp.zeros((ref.shape[0], height, cols), jnp.float32)

        @pl.when(lat == 0)
        def _():
            clear(low)

        @pl.when(lat == n_lat - 1)
        def _():
            clear(high)

        angle = math.pi * (row.astype(jnp.float32) + 0.5) / total_rows - math.pi / 2
        SC[2] = coriolis_scale * jnp.sin(angle)

        def remote(src, dst, send, recv, i, to_lat, to_lon):
            return pltpu.make_async_remote_copy(
                src_ref=src, dst_ref=dst, send_sem=send.at[i], recv_sem=recv.at[i],
                device_id={"lat": to_lat, "lon": to_lon}, device_id_type=MESH,
            )

        def filler(count):
            height = max(h for h in range(1, wide + 1) if count % h == 0)
            return ST.at[pl.ds(0, count // height), pl.ds(0, height)]

        class Group:
            def __init__(self, both, up, down, sends, recvs, counts):
                self.copies, self.sends, self.recvs, self.counts = (both, up, down), sends, recvs, counts

            def each(self, action, toward):
                both, up, down = range(3)
                if self.copies[both]:
                    action(both)
                pl.when(lat < n_lat - 1 if toward else lat > 0)(lambda: action(up))
                pl.when(lat > 0 if toward else lat < n_lat - 1)(lambda: action(down))

            def start(self):
                def go(i):
                    for c in self.copies[i]:
                        c.start()

                self.each(go, True)

            def wait(self, sems, toward):
                def done(i):
                    some = filler(self.counts[i])
                    pltpu.make_async_copy(some, some, sems.at[i]).wait()

                self.each(done, toward)

            def finish_recv(self):
                self.wait(self.recvs, False)

            def finish_send(self):
                self.wait(self.sends, True)

        low_rim, high_rim = pl.ds(PAD - RIM, RIM), pl.ds(PAD + rows, RIM)
        top, bottom = pl.ds(rows - RIM, RIM), pl.ds(0, RIM)

        def strip_copies(to_e, to_w, from_e, from_w, send, recv):
            both = [
                remote(to_e, from_w.at[:, mid_rows, :], send, recv, 0, lat, eastward),
                remote(to_w, from_e.at[:, mid_rows, :], send, recv, 0, lat, westward),
            ]
            up = [
                remote(to_e.at[:, top, :], from_w.at[:, low_rim, :], send, recv, 1, lat + 1, eastward),
                remote(to_w.at[:, top, :], from_e.at[:, low_rim, :], send, recv, 1, lat + 1, westward),
            ]
            down = [
                remote(to_e.at[:, bottom, :], from_w.at[:, high_rim, :], send, recv, 2, lat - 1, eastward),
                remote(to_w.at[:, bottom, :], from_e.at[:, high_rim, :], send, recv, 2, lat - 1, westward),
            ]
            return both, up, down

        def rims(src, dst, i, to_lat):
            return [
                remote(fa.at[:, :, src, :], A0.at[:, inner, dst, :], halo_send, halo_recv, i, to_lat, lon),
                remote(du.at[:, src, :], ST.at[pl.ds(0, levels), dst, :], halo_send, halo_recv, i, to_lat, lon),
                remote(dv.at[:, src, :], ST.at[pl.ds(levels, levels), dst, :], halo_send, halo_recv, i, to_lat, lon),
                remote(wm.at[:, src, :], WI.at[:, dst, :], halo_send, halo_recv, i, to_lat, lon),
                remote(bl.at[src, :], BI.at[dst, :], halo_send, halo_recv, i, to_lat, lon),
                remote(vi.at[src, :], ST.at[misc, dst, :], halo_send, halo_recv, i, to_lat, lon),
                remote(br.at[:, src, :], ST.at[pl.ds(misc + 2, fields), dst, :], halo_send, halo_recv, i, to_lat, lon),
            ]

        planes = (fields + 3) * levels + 2 + fields
        halo = Group(
            [], rims(top, low_rim, 1, lat + 1), rims(bottom, high_rim, 2, lat - 1),
            halo_send, halo_recv, (0, planes * RIM, planes * RIM),
        )
        side = Group(
            *strip_copies(ME, MW, RE, RW, side_send, side_recv), side_send, side_recv,
            (2 * messages * rows, 2 * messages * RIM, 2 * messages * RIM),
        )

        def across(x):
            return jnp.concatenate([x] * 4, axis=0).T

        def by_block(t, which):
            height = t.shape[0] // 4
            x = t[:height]
            for r in range(1, 4):
                x = jnp.where(which == r, t[r * height : (r + 1) * height], x)
            return x

        part_of = (lane[:lines] & (q_share - 1)) // per
        part_block = block[:lines]

        def pack_forcing(step, e, i):
            for b in range(n_lat):
                x = at[step, :, b * s_share : (b + 1) * s_share, :].reshape(lines, cols)
                Y[b] = across(x)
                for p in range(per):
                    x = Y[b, pl.ds(p, n_lon, stride=q_share), :]
                    for r in range(1, 4):
                        x = jnp.where(block[:n_lon] == r, Y[b, pl.ds(per * r + p, n_lon, stride=q_share), :], x)
                    SB[e, pl.ds(b * n_lon * 8 + i * per + p, n_lon, stride=8), :] = x

        def unpack_forcing(e, i, to):
            for b in range(n_lat):
                x = jnp.concatenate(
                    [RB[e, pl.ds(b * n_lon * 8 + i * per + p, n_lon, stride=8), :] for p in range(per)], axis=0
                )
                to[pl.ds(b, lines, stride=n_lat), :] = by_block(across(x), part_block)

        def pack_flux(e, i):
            for b in range(n_lat):
                x = by_block(across(FL[pl.ds(b, lines, stride=n_lat), :]), block[:BLOCK])
                for p in range(per):
                    at_row = b * n_lon * 8 + i * per + p
                    SB[e, pl.ds(at_row, n_lon, stride=8), :] = x[p * n_lon : (p + 1) * n_lon]

        def unpack_flux(e, i, step):
            for b in range(n_lat):
                for p in range(per):
                    x = RB[e, pl.ds(b * n_lon * 8 + i * per + p, n_lon, stride=8), :]
                    for r in range(4):
                        Y[b, pl.ds(per * r + p, n_lon, stride=q_share), :] = x
                x = by_block(Y[b].T, part_of)
                flux[step, :, b * s_share : (b + 1) * s_share, :] = x.reshape(fields, s_share, cols)

        def place_of(device, size):
            return pl.ds(pl.multiple_of(device * 8, 8), size)

        def exchange(e, size):
            def send(la, lo):
                pltpu.make_async_remote_copy(
                    src_ref=SB.at[e, place_of(la * n_lon + lo, size)], dst_ref=RB.at[e, place_of(me, size)],
                    send_sem=a2a_send.at[e], recv_sem=a2a_recv.at[e],
                    device_id={"lat": la, "lon": lo}, device_id_type=MESH,
                ).start()

            for dl in range(n_lat):
                la = lax.rem(lat + dl, n_lat)
                least = 1 if dl == 0 else 0
                if n_lon <= 8:
                    for dn in range(least, n_lon):
                        send(la, lax.rem(lon + dn, n_lon))
                else:
                    @pl.loop(least, n_lon)
                    def _(dn):
                        send(la, lax.rem(lon + dn, n_lon))

            RB[e, place_of(me, 8), :] = SB[e, place_of(me, 8), :]

        def all_of(e, size, sem):
            some = pl.ds(0, (n - 1) * size)
            pltpu.make_async_copy(SB.at[e, some], RB.at[e, some], sem.at[e]).wait()

        loads[0].wait()
        pack_forcing(2, 0, 0)
        pack_forcing(1, 0, 1)

        def convert(part):
            for k in range(levels):
                ST[k, part, :] = 0.5 * ST[k, part, :]
                ST[levels + k, part, :] = 0.5 * ST[levels + k, part, :]
                ST[2 * levels + k, part, :] = WI[k, part, :].astype(jnp.float32)
            ST[misc + 1, part, :] = BI[part, :].astype(jnp.float32)

        def sources(i, part):
            if i < fields * groups:
                f, j = divmod(i, groups)
                return [A0[f, b * groups + j + 1, part, :] for b in range(4)]
            if i < (fields + 3) * groups:
                kind, j = divmod(i - fields * groups, groups)
                return [ST[kind * levels + b * groups + j, part, :] for b in range(4)]
            if i == (fields + 3) * groups:
                v, d = ST[misc, part, :], ST[misc + 1, part, :]
                return [v, d, v, d]
            return [ST[misc + 2 + f, part, :] for f in range(4)]

        loads[1].wait()
        some = filler((3 * levels + 2 + fields) * rows)
        pltpu.make_async_copy(some, some, in_sem.at[2]).wait()
        convert(own)
        for m in range(messages):
            ids = range(4 * m, min(4 * m + 4, strips))
            packed = [pack(sources(i, own)) for i in ids]
            ME[m] = message(packed, 4)
            MW[m] = message(packed, 10)
            for i, x in zip(ids, packed):
                SP[i, own, :] = lay(x)
        pl.semaphore_wait(barrier, n - 1)
        exchange(0, 2 * per)

        side.start()
        halo.start()

        def store_flux(A):
            for f in range(fields):
                FL[f * rows : (f + 1) * rows] = A[f, 1, own, :] * ST[2 * levels, own, :]

        pack_forcing(0, 1, 0)
        store_flux(A0)
        pack_flux(1, 1)

        halo.finish_recv()
        for part in (low, high):
            convert(part)
            for i in range(strips):
                SP[i, part, :] = lay(pack(sources(i, part)))

        all_of(0, 2 * per, a2a_recv)
        for i in range(2):
            unpack_forcing(0, i, FL)
            for f in range(fields):
                F[i * fields + f, own, :] = FL[f * rows : (f + 1) * rows]
        packed = [pack([F[i * fields + f, own, :] for f in range(4)]) for i in range(2)]
        FE[0] = message(packed, 4)
        FW[0] = message(packed, 10)
        both, up, down = strip_copies(FE, FW, FRE, FRW, f_send, f_recv)
        up = up + [remote(F.at[:, pl.ds(PAD + rows - RIM, RIM), :], F.at[:, low_rim, :], f_send, f_recv, 1, lat + 1, lon)]
        down = down + [remote(F.at[:, pl.ds(PAD, RIM), :], F.at[:, high_rim, :], f_send, f_recv, 2, lat - 1, lon)]
        f_halo = Group(
            both, up, down, f_send, f_recv, (2 * rows, (2 + 2 * fields) * RIM, (2 + 2 * fields) * RIM),
        )
        f_halo.start()
        side.finish_recv()
        between = (place >= 10) & (place < 22)
        half = lane & 15
        for m in range(messages):
            from_e, from_w = RE[m], roll_lanes(RW[m], 6)
            even = jnp.where(half < 6, from_e, from_w)
            odd = jnp.where((half >= 8) & (half < 14), from_e, from_w)
            for p in range(min(4, strips - 4 * m)):
                x = roll_lanes((even, odd)[p % 2], 10 - 8 * p)
                SP[4 * m + p] = jnp.where(between, x, SP[4 * m + p])

        strip_u, strip_v, strip_wet = [(fields + i) * groups for i in range(3)]
        x = SP[(fields + 3) * groups]
        SC[0] = jnp.where((block & 1) == 0, x, roll_lanes(x, BLOCK))
        SC[1] = jnp.where((block & 1) == 1, x, roll_lanes(x, -BLOCK)) - (block * groups).astype(jnp.float32)
        x = SP[(fields + 3) * groups + 1]
        for f in range(fields):
            SG[f] = jnp.where(block == 0, SP[strip_wet] * roll_lanes(x, -BLOCK * f), 0.0)

        half_t = 0.5 * pressure_weight * expansion
        half_s = -0.5 * pressure_weight * contraction
        edge2 = (lane < 2) | (lane >= cols - 2)
        edge4 = (lane < 4) | (lane >= cols - 4)
        keep_low = jnp.where(lat > 0, 1.0, 0.0)
        keep_high = jnp.where(lat < n_lat - 1, 1.0, 0.0)

        def masked(x):
            return jnp.concatenate([x[low] * keep_low, x[own], x[high] * keep_high], axis=0)

        def spatial(w, u, v, extra_u, extra_v, visc, part):
            y = visc * w
            inner_lap = (north(y) + south(y)) - 4.0 * y
            z = lap_weight * w - masked(inner_lap)
            along, across = u * w, v * w
            if extra_u is not None:
                along, across = along + extra_u, across + extra_v
            vertical = north(z + across) + south(z - across)
            z, y, along = z[part], y[part], along[part]
            t = z - inner_lap[part]
            flat = (east(t + along) + west(t - along)) - (roll_lanes(y, -2) + roll_lanes(y, 2))
            return (flat + vertical[part]) - (4.0 * z + 2.0 * y)

        def strip_step(A, B):
            depth, visc, cor = SC[1], SC[0], SC[2]
            w = [[SP[strip_wet + j] * A[f * groups + j] for j in range(groups)] for f in range(fields)]
            sums = []
            for f in (2, 3):
                c = [w[f][groups - 1]]
                for j in range(groups - 2, -1, -1):
                    c.insert(0, c[0] + w[f][j])
                later = 0.0
                for b in range(1, 4):
                    later = later + jnp.where(block < 4 - b, roll_lanes(c[0], -BLOCK * b), 0.0)
                sums.append([x + later for x in c])
            down = []
            for j in range(groups):
                mix = jnp.where(depth > j + 1.0, mixing_rate, 0.0)
                down.append([
                    mix * ((w[f][j + 1] if j < groups - 1 else roll_lanes(w[f][0], -BLOCK)) - w[f][j])
                    for f in range(fields)
                ])
            for j in range(groups):
                drag = jnp.where(depth == j + 1.0, drag_rate, 0.0)
                u, v = SP[strip_u + j], SP[strip_v + j]
                for f in range(fields):
                    h = (half_t, half_s, 0.0, 0.0)[f]
                    eu = h * sums[0][j] if f < 2 else None
                    ev = h * sums[1][j] if f < 2 else None
                    x = w[f][j]
                    new = A[f * groups + j] + spatial(x, u, v, eu, ev, visc, everything)
                    up = down[j - 1][f] if j > 0 else roll_lanes(down[groups - 1][f], BLOCK)
                    new = new + (down[j][f] - up)
                    if f == 2:
                        new = new - (drag * x + cor * w[3][j])
                    if f == 3:
                        new = new - (drag * x - cor * w[2][j])
                    B[f * groups + j] = new
                    J[f * groups + j] = jnp.where(place < 10, new, roll_lanes(new, -12))

        wet_top = 2 * levels

        def begin(A):
            wet = ST[wet_top + levels - 1]
            w = [wet * A[f, levels] for f in range(fields)]
            nothing = jnp.zeros((wide, cols), jnp.float32)
            return (nothing, nothing, *w, nothing, nothing, nothing, nothing)

        def level(A, k, carry, part, write):
            cu, cv, *rest = carry
            w, g = rest[:4], rest[4:]
            kf = jnp.asarray(k, jnp.int32).astype(jnp.float32)
            first = kf + jnp.where(k == 0, 1000.0, 0.0)
            depth, visc, cor = ST[misc + 1], ST[misc], SC[2][part]
            wet_up = ST[wet_top + jnp.where(k == 0, 0, k - 1)]
            mix = jnp.where(depth > first, mixing_rate, 0.0)
            drag = jnp.where(depth[part] == kf + 1.0, drag_rate, 0.0)
            u, v = ST[k], ST[levels + k]
            cu, cv = cu + w[2], cv + w[3]
            w_up = [wet_up * A[f, k] for f in range(fields)]
            g_up = [mix * (w[f] - w_up[f]) for f in range(fields)]
            for f in range(fields):
                h = (half_t, half_s, 0.0, 0.0)[f]
                eu = h * cu if f < 2 else None
                ev = h * cv if f < 2 else None
                new = A[f, k + 1][part] + spatial(w[f], u, v, eu, ev, visc, part)
                new = new + (g[f][part] - g_up[f][part])
                if f == 2:
                    new = new - (drag * w[2][part] + cor * w[3][part])
                if f == 3:
                    new = new - (drag * w[3][part] - cor * w[2][part])
                write(f, k, new)
            return (cu, cv, *w_up, *g_up)

        def sweep(A, carry, first, last, part, write):
            def body(i, carry):
                for j in range(UNROLL):
                    carry = level(A, first - i * UNROLL - j, carry, part, write)
                return carry

            return lax.fori_loop(0, (first - last + 1) // UNROLL, body, carry)

        def fixed(f, k, part, edge, new):
            b = k // groups
            x = pltpu.roll(J[f * groups + lax.rem(k, groups), part, :], 118 - BLOCK * b, 1)
            return jnp.where(edge[part], x, new)

        def surface(A, S, B, R, i):
            for f in range(fields):
                R[f * groups] = R[f * groups] + SG[f] * (FS[i * fields + f] - S[f * groups])
                gain = ST[wet_top] * ST[misc + 2 + f]
                B[f, 1] = B[f, 1] + gain * (F[i * fields + f] - A[f, 1])

        exchange(1, 2 * per)
        strip_step(SP, SN)

        def write1(f, k, new):
            A1[f, k + 1] = fixed(f, k, everything, edge2, new)

        sweep(A0, begin(A0), levels - 1, 0, everything, write1)


        def write2(f, k, new):
            A0[f, k + 1] = new

        carry = sweep(A1, begin(A1), levels - 1, groups, everything, write2)

        f_halo.finish_recv()
        for i in range(2):
            x = lay(pack([F[i * fields + f] for f in range(4)]))
            x = jnp.where((place >= 10) & (place < 16), roll_lanes(FRE[0], 10 - 8 * i), x)
            x = jnp.where((place >= 16) & (place < 22), roll_lanes(FRW[0], 16 - 8 * i), x)
            for f in range(fields):
                FS[i * fields + f] = roll_lanes(x, -BLOCK * f)
        surface(A0, SP, A1, SN, 0)
        store_flux(A1)
        pack_flux(2, 0)
        exchange(2, per)
        strip_step(SN, SP)
        sweep(A1, carry, groups - 1, 0, everything, write2)
        for f in range(fields):
            A0[f, 1] = fixed(f, 0, everything, edge2, A0[f, 1])
        surface(A1, SN, A0, SP, 1)
        store_flux(A0)
        pack_flux(3, 0)
        exchange(3, per)

        strip_step(SP, SN)

        def write3(f, k, new):
            out[f, k] = fixed(f, k, own, edge4, new)

        sweep(A0, begin(A0), levels - 1, 0, own, write3)
        all_of(1, 2 * per, a2a_recv)
        unpack_forcing(1, 0, FL)
        for f in range(fields):
            gain = ST[wet_top, own, :] * ST[misc + 2 + f, own, :]
            out[f, 0] = out[f, 0] + gain * (FL[f * rows : (f + 1) * rows] - A0[f, 1, own, :])

        unpack_flux(1, 1, 2)
        all_of(2, per, a2a_recv)
        unpack_flux(2, 0, 1)
        all_of(3, per, a2a_recv)
        unpack_flux(3, 0, 0)
        halo.finish_send()
        side.finish_send()
        f_halo.finish_send()
        for e in range(4):
            all_of(e, (2 * per, 2 * per, per, per)[e], a2a_send)

    return kernel


def local(
    final_adjoint, drift_u, drift_v, wet_mask, bottom_level, viscosity, bulk_rate, atmos_adjoint
):
    fields, levels, rows, cols = final_adjoint.shape
    window = atmos_adjoint.shape[0]
    n_lat, n_lon = lax.axis_size("lat"), lax.axis_size("lon")
    n = n_lat * n_lon
    wide = rows + 2 * PAD
    q_share = cols // n_lon
    groups = levels // 4
    strips = (fields + 3) * groups + 2
    messages = -(-strips // 4)

    def buf(*shape):
        return pltpu.VMEM(shape, jnp.float32)

    kernel = make_kernel(n_lat, n_lon, fields, levels, rows, cols, window, q_share)
    f32 = jnp.float32
    anywhere = pl.BlockSpec(memory_space=pl.ANY)
    return pl.pallas_call(
        kernel,
        out_shape=(
            pltpu.VMEM(final_adjoint.shape, f32),
            pltpu.VMEM(atmos_adjoint.shape, f32),
        ),
        in_specs=[anywhere] * 8,
        out_specs=(pl.BlockSpec(memory_space=pltpu.VMEM),) * 2,
        scratch_shapes=[
            buf(window, fields, rows, cols),
            buf(fields, levels + 1, wide, cols), buf(fields, levels + 1, wide, cols),
            buf(3 * levels + 2 + fields, wide, cols),
            pltpu.VMEM((levels, wide, cols), jnp.int32), pltpu.VMEM((wide, cols), jnp.int32),
            buf(strips, wide, cols), buf(fields * groups, wide, cols),
            buf(3, wide, cols), buf(fields, wide, cols), buf(fields * groups, wide, cols),
            buf(messages, rows, cols), buf(messages, rows, cols),
            buf(messages, wide, cols), buf(messages, wide, cols),
            buf(2 * fields, wide, cols), buf(2 * fields, wide, cols),
            buf(1, rows, cols), buf(1, rows, cols), buf(1, wide, cols), buf(1, wide, cols),
            buf(n_lat, cols, cols), buf(fields * rows, cols), buf(4, n * 8, cols), buf(4, n * 8, cols),
            *[pltpu.SemaphoreType.DMA((3,))] * 6,
            pltpu.SemaphoreType.DMA((4,)), pltpu.SemaphoreType.DMA((4,)), pltpu.SemaphoreType.DMA((3,)),
        ],
        compiler_params=pltpu.CompilerParams(
            collective_id=0, has_side_effects=True, vmem_limit_bytes=60 * 1024 * 1024
        ),
    )(final_adjoint, drift_u, drift_v, wet_mask, bottom_level, viscosity, bulk_rate, atmos_adjoint)


def solution(mesh):
    in_specs = (
        P(None, None, "lat", "lon"),
        P(None, "lat", "lon"),
        P(None, "lat", "lon"),
        P(None, "lat", "lon"),
        P("lat", "lon"),
        P("lat", "lon"),
        P(None, "lat", "lon"),
        P(None, None, "lat", "lon"),
    )
    out_specs = (P(None, None, "lat", "lon"), P(None, None, "lat", "lon"))
    return jax.shard_map(local, mesh=mesh, in_specs=in_specs, out_specs=out_specs, check_vma=False)
```

```python
import math

import jax
import jax.numpy as jnp
from jax import lax
from jax.experimental import pallas as pl
from jax.experimental.pallas import tpu as pltpu
from jax.sharding import PartitionSpec as P

lap_weight = 0.04
mixing_rate = 0.15
drag_rate = 0.2
expansion = 0.2
contraction = 0.15
pressure_weight = 0.1
coriolis_scale = 0.2

MESH = pl.DeviceIdType.MESH
PAD = 8
RIM = 6
BLOCK = 32
UNROLL = 3


def roll_lanes(x, shift):
    shift = shift % x.shape[-1]
    return pltpu.roll(x, shift, x.ndim - 1) if shift else x


def east(x):
    return roll_lanes(x, -1)


def west(x):
    return roll_lanes(x, 1)


def north(x):
    return pltpu.roll(x, x.shape[0] - 1, 0)


def south(x):
    return pltpu.roll(x, 1, 0)


def make_kernel(n_lat, n_lon, fields, levels, rows, cols, window, q_share):
    n = n_lat * n_lon
    wide = rows + 2 * PAD
    total_rows = rows * n_lat
    s_share = rows // n_lat
    lines = fields * s_share
    per = BLOCK // n_lon
    misc = 3 * levels
    groups = levels // 4
    strips = (fields + 3) * groups + 2
    messages = -(-strips // 4)

    def kernel(
        fa, du, dv, wm, bl, vi, br, at_hbm,
        out, flux,
        at, A0, A1, ST, WI, BI, SP, SN, SC, SG, J, ME, MW, RE, RW, F, FS, FE, FW, FRE, FRW,
        Y, FL, SB, RB,
        halo_send, halo_recv, side_send, side_recv, f_send, f_recv, a2a_send, a2a_recv, in_sem,
    ):
        lat = lax.axis_index("lat")
        lon = lax.axis_index("lon")
        me = lat * n_lon + lon
        eastward = lax.rem(lon + 1, n_lon)
        westward = lax.rem(lon + n_lon - 1, n_lon)

        mid_rows = pl.ds(PAD, rows)
        inner = pl.ds(1, levels)
        loads = [
            pltpu.make_async_copy(src, dst, in_sem.at[min(i, 2)])
            for i, (src, dst) in enumerate([
                (at_hbm, at),
                (fa, A0.at[:, inner, mid_rows, :]),
                (du, ST.at[pl.ds(0, levels), mid_rows, :]),
                (dv, ST.at[pl.ds(levels, levels), mid_rows, :]),
                (wm, WI.at[:, mid_rows, :]),
                (bl, BI.at[mid_rows, :]),
                (vi, ST.at[misc, mid_rows, :]),
                (br, ST.at[pl.ds(misc + 2, fields), mid_rows, :]),
            ])
        ]
        for c in loads:
            c.start()

        barrier = pltpu.get_barrier_semaphore()

        def greet(la, lo):
            pl.semaphore_signal(barrier, inc=1, device_id={"lat": la, "lon": lo}, device_id_type=MESH)

        for dl in range(n_lat):
            la = lax.rem(lat + dl, n_lat)
            least = 1 if dl == 0 else 0
            if n_lon <= 8:
                for dn in range(least, n_lon):
                    greet(la, lax.rem(lon + dn, n_lon))
            else:
                @pl.loop(least, n_lon)
                def _(dn):
                    greet(la, lax.rem(lon + dn, n_lon))

        lane = lax.broadcasted_iota(jnp.int32, (wide, cols), 1)
        place = lane & (BLOCK - 1)
        block = lane >> (BLOCK.bit_length() - 1)
        row = lax.broadcasted_iota(jnp.int32, (wide, cols), 0) + lat * rows - PAD
        own = slice(PAD, PAD + rows)
        low = slice(0, PAD)
        high = slice(PAD + rows, wide)
        everything = slice(0, wide)

        def pack(planes):
            height = planes[0].shape[0]
            b = block[:height]
            x = roll_lanes(planes[0], -118)
            for f in range(1, 4):
                x = jnp.where(b == f, roll_lanes(planes[f], BLOCK * f - 118), x)
            return x

        def message(packed, base):
            height = packed[0].shape[0]
            p = place[:height] // 8
            x = roll_lanes(packed[0], -base)
            for j in range(1, len(packed)):
                x = jnp.where(p == j, roll_lanes(packed[j], 8 * j - base), x)
            return x

        def lay(packed):
            return jnp.where(place[: packed.shape[0]] < 10, packed, roll_lanes(packed, 12))

        for ref in (A0, A1):
            ref[:, 0:1] = jnp.zeros((fields, 1, wide, cols), jnp.float32)

        def clear(part):
            A0[:, 1 : levels + 1, part, :] = jnp.zeros((fields, levels, PAD, cols), jnp.float32)
            ST[:, part, :] = jnp.zeros((misc + 2 + fields, PAD, cols), jnp.float32)
            WI[:, part, :] = jnp.zeros((levels, PAD, cols), jnp.int32)
            BI[part, :] = jnp.zeros((PAD, cols), jnp.int32)
            F[:, part, :] = jnp.zeros((2 * fields, PAD, cols), jnp.float32)
            for ref in (RE, RW, FRE, FRW):
                ref[:, part, :] = jnp.zeros((ref.shape[0], PAD, cols), jnp.float32)

        for part in (slice(0, PAD - RIM), slice(PAD + rows + RIM, wide)):
            height = part.stop - part.start
            A0[:, 1 : levels + 1, part, :] = jnp.zeros((fields, levels, height, cols), jnp.float32)
            ST[:, part, :] = jnp.zeros((misc + 2 + fields, height, cols), jnp.float32)
            WI[:, part, :] = jnp.zeros((levels, height, cols), jnp.int32)
            BI[part, :] = jnp.zeros((height, cols), jnp.int32)
            F[:, part, :] = jnp.zeros((2 * fields, height, cols), jnp.float32)
            for ref in (RE, RW, FRE, FRW):
                ref[:, part, :] = jnp.zeros((ref.shape[0], height, cols), jnp.float32)

        @pl.when(lat == 0)
        def _():
            clear(low)

        @pl.when(lat == n_lat - 1)
        def _():
            clear(high)

        angle = math.pi * (row.astype(jnp.float32) + 0.5) / total_rows - math.pi / 2
        SC[2] = coriolis_scale * jnp.sin(angle)

        def remote(src, dst, send, recv, i, to_lat, to_lon):
            return pltpu.make_async_remote_copy(
                src_ref=src, dst_ref=dst, send_sem=send.at[i], recv_sem=recv.at[i],
                device_id={"lat": to_lat, "lon": to_lon}, device_id_type=MESH,
            )

        def filler(count):
            height = max(h for h in range(1, wide + 1) if count % h == 0)
            return ST.at[pl.ds(0, count // height), pl.ds(0, height)]

        class Group:
            def __init__(self, both, up, down, sends, recvs, counts):
                self.copies, self.sends, self.recvs, self.counts = (both, up, down), sends, recvs, counts

            def each(self, action, toward):
                both, up, down = range(3)
                if self.copies[both]:
                    action(both)
                pl.when(lat < n_lat - 1 if toward else lat > 0)(lambda: action(up))
                pl.when(lat > 0 if toward else lat < n_lat - 1)(lambda: action(down))

            def start(self):
                def go(i):
                    for c in self.copies[i]:
                        c.start()

                self.each(go, True)

            def wait(self, sems, toward):
                def done(i):
                    some = filler(self.counts[i])
                    pltpu.make_async_copy(some, some, sems.at[i]).wait()

                self.each(done, toward)

            def finish_recv(self):
                self.wait(self.recvs, False)

            def finish_send(self):
                self.wait(self.sends, True)

        low_rim, high_rim = pl.ds(PAD - RIM, RIM), pl.ds(PAD + rows, RIM)
        top, bottom = pl.ds(rows - RIM, RIM), pl.ds(0, RIM)

        def strip_copies(to_e, to_w, from_e, from_w, send, recv):
            both = [
                remote(to_e, from_w.at[:, mid_rows, :], send, recv, 0, lat, eastward),
                remote(to_w, from_e.at[:, mid_rows, :], send, recv, 0, lat, westward),
            ]
            up = [
                remote(to_e.at[:, top, :], from_w.at[:, low_rim, :], send, recv, 1, lat + 1, eastward),
                remote(to_w.at[:, top, :], from_e.at[:, low_rim, :], send, recv, 1, lat + 1, westward),
            ]
            down = [
                remote(to_e.at[:, bottom, :], from_w.at[:, high_rim, :], send, recv, 2, lat - 1, eastward),
                remote(to_w.at[:, bottom, :], from_e.at[:, high_rim, :], send, recv, 2, lat - 1, westward),
            ]
            return both, up, down

        def rims(src, dst, i, to_lat):
            return [
                remote(fa.at[:, :, src, :], A0.at[:, inner, dst, :], halo_send, halo_recv, i, to_lat, lon),
                remote(du.at[:, src, :], ST.at[pl.ds(0, levels), dst, :], halo_send, halo_recv, i, to_lat, lon),
                remote(dv.at[:, src, :], ST.at[pl.ds(levels, levels), dst, :], halo_send, halo_recv, i, to_lat, lon),
                remote(wm.at[:, src, :], WI.at[:, dst, :], halo_send, halo_recv, i, to_lat, lon),
                remote(bl.at[src, :], BI.at[dst, :], halo_send, halo_recv, i, to_lat, lon),
                remote(vi.at[src, :], ST.at[misc, dst, :], halo_send, halo_recv, i, to_lat, lon),
                remote(br.at[:, src, :], ST.at[pl.ds(misc + 2, fields), dst, :], halo_send, halo_recv, i, to_lat, lon),
            ]

        planes = (fields + 3) * levels + 2 + fields
        halo = Group(
            [], rims(top, low_rim, 1, lat + 1), rims(bottom, high_rim, 2, lat - 1),
            halo_send, halo_recv, (0, planes * RIM, planes * RIM),
        )
        side = Group(
            *strip_copies(ME, MW, RE, RW, side_send, side_recv), side_send, side_recv,
            (2 * messages * rows, 2 * messages * RIM, 2 * messages * RIM),
        )

        def across(x):
            return jnp.concatenate([x] * 4, axis=0).T

        def by_block(t, which):
            height = t.shape[0] // 4
            x = t[:height]
            for r in range(1, 4):
                x = jnp.where(which == r, t[r * height : (r + 1) * height], x)
            return x

        part_of = (lane[:lines] & (q_share - 1)) // per
        part_block = block[:lines]

        def pack_forcing(step, e, i):
            for b in range(n_lat):
                x = at[step, :, b * s_share : (b + 1) * s_share, :].reshape(lines, cols)
                Y[b] = across(x)
                for p in range(per):
                    x = Y[b, pl.ds(p, n_lon, stride=q_share), :]
                    for r in range(1, 4):
                        x = jnp.where(block[:n_lon] == r, Y[b, pl.ds(per * r + p, n_lon, stride=q_share), :], x)
                    SB[e, pl.ds(b * n_lon * 8 + i * per + p, n_lon, stride=8), :] = x

        def unpack_forcing(e, i, to):
            for b in range(n_lat):
                x = jnp.concatenate(
                    [RB[e, pl.ds(b * n_lon * 8 + i * per + p, n_lon, stride=8), :] for p in range(per)], axis=0
                )
                to[pl.ds(b, lines, stride=n_lat), :] = by_block(across(x), part_block)

        def pack_flux(e, i):
            for b in range(n_lat):
                x = by_block(across(FL[pl.ds(b, lines, stride=n_lat), :]), block[:BLOCK])
                for p in range(per):
                    at_row = b * n_lon * 8 + i * per + p
                    SB[e, pl.ds(at_row, n_lon, stride=8), :] = x[p * n_lon : (p + 1) * n_lon]

        def unpack_flux(e, i, step):
            for b in range(n_lat):
                for p in range(per):
                    x = RB[e, pl.ds(b * n_lon * 8 + i * per + p, n_lon, stride=8), :]
                    for r in range(4):
                        Y[b, pl.ds(per * r + p, n_lon, stride=q_share), :] = x
                x = by_block(Y[b].T, part_of)
                flux[step, :, b * s_share : (b + 1) * s_share, :] = x.reshape(fields, s_share, cols)

        def place_of(device, size):
            return pl.ds(pl.multiple_of(device * 8, 8), size)

        def exchange(e, size):
            def send(la, lo):
                pltpu.make_async_remote_copy(
                    src_ref=SB.at[e, place_of(la * n_lon + lo, size)], dst_ref=RB.at[e, place_of(me, size)],
                    send_sem=a2a_send.at[e], recv_sem=a2a_recv.at[e],
                    device_id={"lat": la, "lon": lo}, device_id_type=MESH,
                ).start()

            for dl in range(n_lat):
                la = lax.rem(lat + dl, n_lat)
                least = 1 if dl == 0 else 0
                if n_lon <= 8:
                    for dn in range(least, n_lon):
                        send(la, lax.rem(lon + dn, n_lon))
                else:
                    @pl.loop(least, n_lon)
                    def _(dn):
                        send(la, lax.rem(lon + dn, n_lon))

            RB[e, place_of(me, 8), :] = SB[e, place_of(me, 8), :]

        def all_of(e, size, sem):
            some = pl.ds(0, (n - 1) * size)
            pltpu.make_async_copy(SB.at[e, some], RB.at[e, some], sem.at[e]).wait()

        loads[0].wait()
        pack_forcing(2, 0, 0)
        pack_forcing(1, 0, 1)

        def convert(part):
            for k in range(levels):
                ST[k, part, :] = 0.5 * ST[k, part, :]
                ST[levels + k, part, :] = 0.5 * ST[levels + k, part, :]
                ST[2 * levels + k, part, :] = WI[k, part, :].astype(jnp.float32)
            ST[misc + 1, part, :] = BI[part, :].astype(jnp.float32)

        def sources(i, part):
            if i < fields * groups:
                f, j = divmod(i, groups)
                return [A0[f, b * groups + j + 1, part, :] for b in range(4)]
            if i < (fields + 3) * groups:
                kind, j = divmod(i - fields * groups, groups)
                return [ST[kind * levels + b * groups + j, part, :] for b in range(4)]
            if i == (fields + 3) * groups:
                v, d = ST[misc, part, :], ST[misc + 1, part, :]
                return [v, d, v, d]
            return [ST[misc + 2 + f, part, :] for f in range(4)]

        loads[1].wait()
        some = filler((3 * levels + 2 + fields) * rows)
        pltpu.make_async_copy(some, some, in_sem.at[2]).wait()
        convert(own)
        for m in range(messages):
            ids = range(4 * m, min(4 * m + 4, strips))
            packed = [pack(sources(i, own)) for i in ids]
            ME[m] = message(packed, 4)
            MW[m] = message(packed, 10)
            for i, x in zip(ids, packed):
                SP[i, own, :] = lay(x)
        pl.semaphore_wait(barrier, n - 1)
        exchange(0, 2 * per)

        side.start()
        halo.start()

        def store_flux(A):
            for f in range(fields):
                FL[f * rows : (f + 1) * rows] = A[f, 1, own, :] * ST[2 * levels, own, :]

        pack_forcing(0, 1, 0)
        store_flux(A0)
        pack_flux(1, 1)

        halo.finish_recv()
        for part in (low, high):
            convert(part)
            for i in range(strips):
                SP[i, part, :] = lay(pack(sources(i, part)))

        all_of(0, 2 * per, a2a_recv)
        for i in range(2):
            unpack_forcing(0, i, FL)
            for f in range(fields):
                F[i * fields + f, own, :] = FL[f * rows : (f + 1) * rows]
        packed = [pack([F[i * fields + f, own, :] for f in range(4)]) for i in range(2)]
        FE[0] = message(packed, 4)
        FW[0] = message(packed, 10)
        both, up, down = strip_copies(FE, FW, FRE, FRW, f_send, f_recv)
        up = up + [remote(F.at[:, pl.ds(PAD + rows - RIM, RIM), :], F.at[:, low_rim, :], f_send, f_recv, 1, lat + 1, lon)]
        down = down + [remote(F.at[:, pl.ds(PAD, RIM), :], F.at[:, high_rim, :], f_send, f_recv, 2, lat - 1, lon)]
        f_halo = Group(
            both, up, down, f_send, f_recv, (2 * rows, (2 + 2 * fields) * RIM, (2 + 2 * fields) * RIM),
        )
        f_halo.start()
        side.finish_recv()
        between = (place >= 10) & (place < 22)
        half = lane & 15
        for m in range(messages):
            from_e, from_w = RE[m], roll_lanes(RW[m], 6)
            even = jnp.where(half < 6, from_e, from_w)
            odd = jnp.where((half >= 8) & (half < 14), from_e, from_w)
            for p in range(min(4, strips - 4 * m)):
                x = roll_lanes((even, odd)[p % 2], 10 - 8 * p)
                SP[4 * m + p] = jnp.where(between, x, SP[4 * m + p])

        strip_u, strip_v, strip_wet = [(fields + i) * groups for i in range(3)]
        x = SP[(fields + 3) * groups]
        SC[0] = jnp.where((block & 1) == 0, x, roll_lanes(x, BLOCK))
        SC[1] = jnp.where((block & 1) == 1, x, roll_lanes(x, -BLOCK)) - (block * groups).astype(jnp.float32)
        x = SP[(fields + 3) * groups + 1]
        for f in range(fields):
            SG[f] = jnp.where(block == 0, SP[strip_wet] * roll_lanes(x, -BLOCK * f), 0.0)

        half_t = 0.5 * pressure_weight * expansion
        half_s = -0.5 * pressure_weight * contraction
        edge2 = (lane < 2) | (lane >= cols - 2)
        edge4 = (lane < 4) | (lane >= cols - 4)
        keep_low = jnp.where(lat > 0, 1.0, 0.0)
        keep_high = jnp.where(lat < n_lat - 1, 1.0, 0.0)

        def masked(x):
            return jnp.concatenate([x[low] * keep_low, x[own], x[high] * keep_high], axis=0)

        def spatial(w, u, v, extra_u, extra_v, visc, part):
            y = visc * w
            inner_lap = (north(y) + south(y)) - 4.0 * y
            z = lap_weight * w - masked(inner_lap)
            along, across = u * w, v * w
            if extra_u is not None:
                along, across = along + extra_u, across + extra_v
            vertical = north(z + across) + south(z - across)
            z, y, along = z[part], y[part], along[part]
            t = z - inner_lap[part]
            flat = (east(t + along) + west(t - along)) - (roll_lanes(y, -2) + roll_lanes(y, 2))
            return (flat + vertical[part]) - (4.0 * z + 2.0 * y)

        def strip_step(A, B):
            depth, visc, cor = SC[1], SC[0], SC[2]
            w = [[SP[strip_wet + j] * A[f * groups + j] for j in range(groups)] for f in range(fields)]
            sums = []
            for f in (2, 3):
                c = [w[f][groups - 1]]
                for j in range(groups - 2, -1, -1):
                    c.insert(0, c[0] + w[f][j])
                later = 0.0
                for b in range(1, 4):
                    later = later + jnp.where(block < 4 - b, roll_lanes(c[0], -BLOCK * b), 0.0)
                sums.append([x + later for x in c])
            down = []
            for j in range(groups):
                mix = jnp.where(depth > j + 1.0, mixing_rate, 0.0)
                down.append([
                    mix * ((w[f][j + 1] if j < groups - 1 else roll_lanes(w[f][0], -BLOCK)) - w[f][j])
                    for f in range(fields)
                ])
            for j in range(groups):
                drag = jnp.where(depth == j + 1.0, drag_rate, 0.0)
                u, v = SP[strip_u + j], SP[strip_v + j]
                for f in range(fields):
                    h = (half_t, half_s, 0.0, 0.0)[f]
                    eu = h * sums[0][j] if f < 2 else None
                    ev = h * sums[1][j] if f < 2 else None
                    x = w[f][j]
                    new = A[f * groups + j] + spatial(x, u, v, eu, ev, visc, everything)
                    up = down[j - 1][f] if j > 0 else roll_lanes(down[groups - 1][f], BLOCK)
                    new = new + (down[j][f] - up)
                    if f == 2:
                        new = new - (drag * x + cor * w[3][j])
                    if f == 3:
                        new = new - (drag * x - cor * w[2][j])
                    B[f * groups + j] = new
                    J[f * groups + j] = jnp.where(place < 10, new, roll_lanes(new, -12))

        wet_top = 2 * levels

        def begin(A):
            wet = ST[wet_top + levels - 1]
            w = [wet * A[f, levels] for f in range(fields)]
            nothing = jnp.zeros((wide, cols), jnp.float32)
            return (nothing, nothing, *w, nothing, nothing, nothing, nothing)

        def level(A, k, carry, part, write):
            cu, cv, *rest = carry
            w, g = rest[:4], rest[4:]
            kf = jnp.asarray(k, jnp.int32).astype(jnp.float32)
            first = kf + jnp.where(k == 0, 1000.0, 0.0)
            depth, visc, cor = ST[misc + 1], ST[misc], SC[2][part]
            wet_up = ST[wet_top + jnp.where(k == 0, 0, k - 1)]
            mix = jnp.where(depth > first, mixing_rate, 0.0)
            drag = jnp.where(depth[part] == kf + 1.0, drag_rate, 0.0)
            u, v = ST[k], ST[levels + k]
            cu, cv = cu + w[2], cv + w[3]
            w_up = [wet_up * A[f, k] for f in range(fields)]
            g_up = [mix * (w[f] - w_up[f]) for f in range(fields)]
            for f in range(fields):
                h = (half_t, half_s, 0.0, 0.0)[f]
                eu = h * cu if f < 2 else None
                ev = h * cv if f < 2 else None
                new = A[f, k + 1][part] + spatial(w[f], u, v, eu, ev, visc, part)
                new = new + (g[f][part] - g_up[f][part])
                if f == 2:
                    new = new - (drag * w[2][part] + cor * w[3][part])
                if f == 3:
                    new = new - (drag * w[3][part] - cor * w[2][part])
                write(f, k, new)
            return (cu, cv, *w_up, *g_up)

        def sweep(A, carry, first, last, part, write):
            def body(i, carry):
                for j in range(UNROLL):
                    carry = level(A, first - i * UNROLL - j, carry, part, write)
                return carry

            return lax.fori_loop(0, (first - last + 1) // UNROLL, body, carry)

        def fixed(f, k, part, edge, new):
            b = k // groups
            x = pltpu.roll(J[f * groups + lax.rem(k, groups), part, :], 118 - BLOCK * b, 1)
            return jnp.where(edge[part], x, new)

        def surface(A, S, B, R, i):
            for f in range(fields):
                R[f * groups] = R[f * groups] + SG[f] * (FS[i * fields + f] - S[f * groups])
                gain = ST[wet_top] * ST[misc + 2 + f]
                B[f, 1] = B[f, 1] + gain * (F[i * fields + f] - A[f, 1])

        exchange(1, 2 * per)
        strip_step(SP, SN)

        def write1(f, k, new):
            A1[f, k + 1] = fixed(f, k, everything, edge2, new)

        sweep(A0, begin(A0), levels - 1, 0, everything, write1)


        def write2(f, k, new):
            A0[f, k + 1] = new

        carry = sweep(A1, begin(A1), levels - 1, groups, everything, write2)

        f_halo.finish_recv()
        for i in range(2):
            x = lay(pack([F[i * fields + f] for f in range(4)]))
            x = jnp.where((place >= 10) & (place < 16), roll_lanes(FRE[0], 10 - 8 * i), x)
            x = jnp.where((place >= 16) & (place < 22), roll_lanes(FRW[0], 16 - 8 * i), x)
            for f in range(fields):
                FS[i * fields + f] = roll_lanes(x, -BLOCK * f)
        surface(A0, SP, A1, SN, 0)
        store_flux(A1)
        pack_flux(2, 0)
        exchange(2, per)
        strip_step(SN, SP)
        sweep(A1, carry, groups - 1, 0, everything, write2)
        for f in range(fields):
            A0[f, 1] = fixed(f, 0, everything, edge2, A0[f, 1])
        surface(A1, SN, A0, SP, 1)
        store_flux(A0)
        pack_flux(3, 0)
        exchange(3, per)

        strip_step(SP, SN)

        def write3(f, k, new):
            out[f, k] = fixed(f, k, own, edge4, new)

        sweep(A0, begin(A0), levels - 1, 0, own, write3)
        all_of(1, 2 * per, a2a_recv)
        unpack_forcing(1, 0, FL)
        for f in range(fields):
            gain = ST[wet_top, own, :] * ST[misc + 2 + f, own, :]
            out[f, 0] = out[f, 0] + gain * (FL[f * rows : (f + 1) * rows] - A0[f, 1, own, :])

        unpack_flux(1, 1, 2)
        all_of(2, per, a2a_recv)
        unpack_flux(2, 0, 1)
        all_of(3, per, a2a_recv)
        unpack_flux(3, 0, 0)
        halo.finish_send()
        side.finish_send()
        f_halo.finish_send()
        for e in range(4):
            all_of(e, (2 * per, 2 * per, per, per)[e], a2a_send)

    return kernel


def local(
    final_adjoint, drift_u, drift_v, wet_mask, bottom_level, viscosity, bulk_rate, atmos_adjoint
):
    fields, levels, rows, cols = final_adjoint.shape
    window = atmos_adjoint.shape[0]
    n_lat, n_lon = lax.axis_size("lat"), lax.axis_size("lon")
    n = n_lat * n_lon
    wide = rows + 2 * PAD
    q_share = cols // n_lon
    groups = levels // 4
    strips = (fields + 3) * groups + 2
    messages = -(-strips // 4)

    def buf(*shape):
        return pltpu.VMEM(shape, jnp.float32)

    kernel = make_kernel(n_lat, n_lon, fields, levels, rows, cols, window, q_share)
    f32 = jnp.float32
    anywhere = pl.BlockSpec(memory_space=pl.ANY)
    return pl.pallas_call(
        kernel,
        out_shape=(
            pltpu.VMEM(final_adjoint.shape, f32),
            pltpu.VMEM(atmos_adjoint.shape, f32),
        ),
        in_specs=[anywhere] * 8,
        out_specs=(pl.BlockSpec(memory_space=pltpu.VMEM),) * 2,
        scratch_shapes=[
            buf(window, fields, rows, cols),
            buf(fields, levels + 1, wide, cols), buf(fields, levels + 1, wide, cols),
            buf(3 * levels + 2 + fields, wide, cols),
            pltpu.VMEM((levels, wide, cols), jnp.int32), pltpu.VMEM((wide, cols), jnp.int32),
            buf(strips, wide, cols), buf(fields * groups, wide, cols),
            buf(3, wide, cols), buf(fields, wide, cols), buf(fields * groups, wide, cols),
            buf(messages, rows, cols), buf(messages, rows, cols),
            buf(messages, wide, cols), buf(messages, wide, cols),
            buf(2 * fields, wide, cols), buf(2 * fields, wide, cols),
            buf(1, rows, cols), buf(1, rows, cols), buf(1, wide, cols), buf(1, wide, cols),
            buf(n_lat, cols, cols), buf(fields * rows, cols), buf(4, n * 8, cols), buf(4, n * 8, cols),
            *[pltpu.SemaphoreType.DMA((3,))] * 6,
            pltpu.SemaphoreType.DMA((4,)), pltpu.SemaphoreType.DMA((4,)), pltpu.SemaphoreType.DMA((3,)),
        ],
        compiler_params=pltpu.CompilerParams(
            collective_id=0, has_side_effects=True, vmem_limit_bytes=60 * 1024 * 1024
        ),
    )(final_adjoint, drift_u, drift_v, wet_mask, bottom_level, viscosity, bulk_rate, atmos_adjoint)


def solution(mesh):
    in_specs = (
        P(None, None, "lat", "lon"),
        P(None, "lat", "lon"),
        P(None, "lat", "lon"),
        P(None, "lat", "lon"),
        P("lat", "lon"),
        P("lat", "lon"),
        P(None, "lat", "lon"),
        P(None, None, "lat", "lon"),
    )
    out_specs = (P(None, None, "lat", "lon"), P(None, None, "lat", "lon"))
    return jax.shard_map(local, mesh=mesh, in_specs=in_specs, out_specs=out_specs, check_vma=False)
```
